32 devices in a mesh: wide: 16 (over z, y, core), narrow: 2 (over x).
Axes of the slice: x: 2, y: 2, z: 4, core: 2. Of those that a mesh axis runs over, the one named last changes fastest.
Arguments:
- tokens: bfloat16 [2048, 2, 1024], P('wide', 'narrow'), may hold values from -6 to 6
- document: int32 [2048, 2], P('wide', 'narrow'), may hold values from 0 to 4, as said below
- routing: int32 [2048, 2, 1], P('wide', 'narrow'), may hold values from 0 to 1
- capacity: int32 [2], replicated, may hold values from 40 to 80
- load_before: float32 [2], replicated, may hold values from 0.5 to 1.5
- first_gain: float32 [1024], replicated, may hold values from 0.5 to 1.5
- first_shift: float32 [1024], replicated, may hold values from -1 to 1
- project_in: bfloat16 [1024, 3072], replicated, may hold values from -0.1875 to 0.1875
- project_out: bfloat16 [1024, 1024], replicated, may hold values from -1.5 to 1.5
- second_gain: float32 [1024], replicated, may hold values from 0.5 to 1.5
- second_shift: float32 [1024], replicated, may hold values from -1 to 1
- dense_up: bfloat16 [1024, 4096], replicated, may hold values from -0.1875 to 0.1875
- dense_down: bfloat16 [4096, 1024], replicated, may hold values from -0.09375 to 0.09375
- router: bfloat16 [1024, 2], replicated, may hold values from -0.125 to 0.125
- mixer: bfloat16 [1024, 2], replicated, may hold values from -0.09375 to 0.09375
- mixer_bias: float32 [2], replicated, may hold values from -2 to 2
- expert_up: bfloat16 [1024, 2, 4096], P(None, 'narrow'), may hold values from -0.1875 to 0.1875
- expert_down: bfloat16 [4096, 2, 1024], P(None, 'narrow'), may hold values from -0.1875 to 0.1875
- cotangent: bfloat16 [2048, 2, 1024], P('wide', 'narrow'), may hold values from -6 to 6
Outputs:
- result: bfloat16 [2048, 2, 1024], P('wide', 'narrow')
- input_grad: bfloat16 [2048, 2, 1024], P('wide', 'narrow')
- first_gain_grad: float32 [1024], P('wide')
- first_shift_grad: float32 [1024], P('wide')
- project_in_grad: float32 [1024, 3072], P('wide')
- project_out_grad: float32 [1024, 1024], P('wide')
- second_gain_grad: float32 [1024], P('wide')
- second_shift_grad: float32 [1024], P('wide')
- dense_up_grad: float32 [1024, 4096], P('wide')
- dense_down_grad: float32 [4096, 1024], P('wide')
- router_grad: float32 [1024, 2], P('wide')
- mixer_grad: float32 [1024, 2], P('wide')
- mixer_bias_grad: float32 [2], replicated
- expert_up_grad: float32 [1024, 2, 4096], P('wide', 'narrow')
- expert_down_grad: float32 [4096, 2, 1024], P('wide', 'narrow')
- load_after: float32 [2], replicated
The draws below stay inside these ranges and needn't reach their ends.
Inputs may be any that keep to these rules, and one draw needn't show every extreme that they name: `document`: along each sequence the numbers never fall.
All inputs are finite; a program needn't handle non-finite values.
Results may differ from the reference program's by a relative error of at most 0.03.
Values may be sent and summed in bfloat16 or wider, within the bound.
No kernel may reach another device: no remote copies, remote signals or barrier semaphores. Data moves between devices by JAX's collectives and lax.ppermute only.
A program may use at most 256 MiB of HBM per device.

```python
import math
import jax
import jax.numpy as jnp
from jax import lax

D = 1024
HEADS = 16
HEAD_DIM = 64
FF = 4096
STRETCH = 128
SEQS = 1
EXPERTS = 2
LEN = 2048
BATCH = 2
CAP = 80
TOKENS = 4096
N_WIDE = 16
N_NARROW = 2


boundary_count = 4


def draw_document(key, part):
    key = jax.random.fold_in(key, 5)
    spread_key, head_key, tail_key, pick_key = jax.random.split(key, 4)
    anywhere = jax.random.randint(spread_key, (BATCH, boundary_count), 1, LEN)
    early = jax.random.randint(head_key, (BATCH, boundary_count), 1, STRETCH)
    late = jax.random.randint(tail_key, (BATCH, boundary_count), LEN - STRETCH + 1, LEN)
    halves = jnp.arange(boundary_count) < boundary_count // 2
    spanning = jnp.where(halves[None, :], early, late)
    picked = jax.random.randint(pick_key, (BATCH // SEQS,), 0, SEQS)
    column = jnp.arange(BATCH)
    is_picked = column % SEQS == jnp.repeat(picked, SEQS)
    bounds = jnp.where(is_picked[:, None], spanning, anywhere)
    positions = jnp.arange(LEN)
    labels = jnp.sum((positions[:, None, None] >= bounds[None, :, :]).astype(jnp.int32), axis=-1)
    return labels.astype(jnp.int32)


def draw_capacity(key, part):
    key = jax.random.fold_in(key, 23)
    value_key, full_key = jax.random.split(key, 2)
    lowest = max(CAP - CAP // 2, 2)
    values = jax.random.randint(value_key, (EXPERTS,), lowest, CAP + 1)
    full_one = jax.random.randint(full_key, (), 0, EXPERTS)
    return jnp.where(jnp.arange(EXPERTS) == full_one, CAP, values).astype(jnp.int32)


def shard_levels(key, dims, pieces, smallest, high):
    factor_of, own = 1.0, jax.random.fold_in(key, 6)
    for position, shards_of in pieces:
        draws = jnp.exp(jax.random.uniform(jax.random.fold_in(own, position), (shards_of,), jnp.float32, smallest / len(pieces), high / len(pieces)))
        factor_of = factor_of * jnp.repeat(draws, dims[position] // shards_of).reshape([-1 if axis == position else 1 for axis in range(len(dims))])
    return factor_of


def distinct(own_key, rows, number_of, top, lift):
    ranking = jax.random.permutation(jax.random.fold_in(own_key, 1), number_of)
    favour = ranking
    for power in range(3):
        favour = favour * favour // number_of
    favour = favour * lift // number_of
    lots = jax.random.randint(jax.random.fold_in(own_key, 2), (rows, number_of), 0, 4096) + favour
    sure = jax.random.permutation(jax.random.fold_in(own_key, 3), rows)[jnp.arange(number_of) % rows]
    lots = jnp.where(jnp.arange(rows)[:, None] == sure[None, :], 1 << 14, lots)
    priority = lots * number_of + jnp.arange(number_of)
    return lax.top_k(priority.astype(jnp.int32), top)[1].astype(jnp.int32)


def gaussian(rng, dims, deviation, most, cuts=(), kind=jnp.bfloat16):
    array = deviation * jax.random.normal(rng, dims, jnp.float32)
    if cuts:
        array = array * shard_levels(rng, dims, cuts, -0.22, 0.18)
    return jnp.clip(array, -most, most).astype(kind)


def setup_inputs(seed: int = 0) -> dict:
    key_list = jax.random.split(jax.random.key(seed), 20)
    return {
        "tokens": gaussian(key_list[0], (LEN, BATCH, D), 1.0, 6.0, ((0, 16), (1, 2))),
        "document": draw_document(jax.random.fold_in(key_list[19], 71), 0),
        "routing": distinct(key_list[2], LEN * BATCH, EXPERTS, 1, 4096).reshape((LEN, BATCH, 1)),
        "capacity": draw_capacity(jax.random.fold_in(key_list[19], 71), 0),
        "load_before": jnp.clip(jax.random.uniform(key_list[4], (EXPERTS,), jnp.float32, 0.5, 1.5), 0.5, 1.5),
        "first_gain": jnp.clip(1.0 + 0.1 * jax.random.normal(key_list[5], (D,), jnp.float32), 0.5, 1.5),
        "first_shift": gaussian(key_list[6], (D,), 0.2, 1.0, (), jnp.float32),
        "project_in": gaussian(key_list[7], (D, 3 * D), D ** -0.5, 0.1875),
        "project_out": gaussian(key_list[8], (D, D), (D // 64) ** -0.5, 1.5),
        "second_gain": jnp.clip(1.0 + 0.1 * jax.random.normal(key_list[9], (D,), jnp.float32), 0.5, 1.5),
        "second_shift": gaussian(key_list[10], (D,), 0.2, 1.0, (), jnp.float32),
        "dense_up": gaussian(key_list[11], (D, FF), D ** -0.5, 0.1875),
        "dense_down": gaussian(key_list[12], (FF, D), FF ** -0.5, 0.09375),
        "router": gaussian(key_list[13], (D, EXPERTS), (2 * D) ** -0.5, 0.125),
        "mixer": gaussian(key_list[14], (D, 2), (4 * D) ** -0.5, 0.09375),
        "mixer_bias": gaussian(key_list[15], (2,), 0.5, 2.0, (), jnp.float32),
        "expert_up": gaussian(key_list[16], (D, EXPERTS, FF), D ** -0.5, 0.1875, ((1, 2),)),
        "expert_down": gaussian(key_list[17], (FF, EXPERTS, D), (FF // (EXPERTS * EXPERTS)) ** -0.5, 0.1875, ((1, 2),)),
        "cotangent": gaussian(key_list[18], (LEN, BATCH, D), 1.0, 6.0, ((0, 16), (1, 2))),
    }


@jax.custom_vjp
def low(v):
    return lax.optimization_barrier(v.astype(jnp.bfloat16)).astype(jnp.float32)

@jax.custom_vjp
def low_back(v):
    return v

def low_keep(v):
    return (low(v), None)

def low_pass(kept, grad):
    return (grad,)

def back_keep(v):
    return (v, None)

def back_low(kept, grad):
    return (low(grad),)
low.defvjp(low_keep, low_pass)
low_back.defvjp(back_keep, back_low)
score_scale = 0.125
norm_eps = 1e-05
momentum = 0.3
masked_score = -1e+30
highest = lax.Precision.HIGHEST

def normalize(inputs, weight_gain, weight_shift):
    average = lax.optimization_barrier(jnp.mean(inputs, axis=-1, keepdims=True))
    centered = inputs - average
    variance = lax.optimization_barrier(jnp.mean(centered * centered, axis=-1, keepdims=True))
    return centered * lax.rsqrt(variance + norm_eps) * weight_gain + weight_shift

def smooth(inputs):
    return jax.nn.gelu(inputs, approximate=True)

def product(left, right):
    return jnp.dot(left, right, precision=highest, preferred_element_type=jnp.float32)

def attend_sequence(projected, labels):
    query_all = projected[:, :D].reshape(LEN, HEADS, HEAD_DIM)
    key_all = projected[:, D:2 * D].reshape(LEN, HEADS, HEAD_DIM)
    value_all = projected[:, 2 * D:].reshape(LEN, HEADS, HEAD_DIM)
    span_rows = math.gcd(LEN, 512)
    places = jnp.arange(LEN, dtype=jnp.int32)

    def one_block(block_index):
        first_row = (block_index * span_rows).astype(jnp.int32)
        query_block = lax.dynamic_slice_in_dim(query_all, first_row, span_rows, 0)
        label_block = lax.dynamic_slice_in_dim(labels, first_row, span_rows, 0)
        scores = low_back(jnp.einsum('qhd,khd->hqk', query_block, key_all, precision=highest) * score_scale)
        query_place = first_row + jnp.arange(span_rows, dtype=jnp.int32)
        allowed = ((places[None, :] <= query_place[:, None]) & (label_block[:, None] == labels[None, :]))[None]
        masked = jnp.where(allowed, scores, masked_score)
        peak = lax.optimization_barrier(jnp.max(masked, axis=-1, keepdims=True))
        weights = jnp.where(allowed, jnp.exp(masked - peak), 0.0)
        probs = low(weights / lax.optimization_barrier(jnp.sum(weights, axis=-1, keepdims=True)))
        return jnp.einsum('hqk,khd->qhd', probs, value_all, precision=highest)
    outputs = lax.map(jax.checkpoint(one_block), jnp.arange(LEN // span_rows, dtype=jnp.int32))
    return outputs.reshape(LEN, D)

def reference(tokens, document, routing, capacity, load_before, first_gain, first_shift, project_in, project_out, second_gain, second_shift, dense_up, dense_down, router, mixer, mixer_bias, expert_up, expert_down, cotangent):
    device_total = N_WIDE * N_NARROW
    chosen = routing[:, :, 0]
    device_view = chosen.reshape(N_WIDE, STRETCH, N_NARROW, SEQS).transpose(0, 2, 1, 3).reshape(N_WIDE, N_NARROW, STRETCH * SEQS)
    onehot = (device_view[..., None] == jnp.arange(EXPERTS, dtype=jnp.int32)).astype(jnp.int32)
    earlier = jnp.cumsum(onehot, axis=2) - onehot
    slot_rank = lax.optimization_barrier(jnp.sum(earlier * onehot, axis=-1))
    limit = lax.optimization_barrier(jnp.sum(capacity * onehot, axis=-1))
    kept = slot_rank < limit
    device_number = (jnp.arange(N_WIDE, dtype=jnp.int32)[:, None] * N_NARROW + jnp.arange(N_NARROW, dtype=jnp.int32)[None, :])[..., None]
    slot_total = EXPERTS * device_total * CAP
    place = jnp.where(kept, device_view * (device_total * CAP) + device_number * CAP + slot_rank, slot_total).astype(jnp.int32)
    place = place.reshape(N_WIDE, N_NARROW, STRETCH, SEQS).transpose(0, 2, 1, 3).reshape(LEN * BATCH).astype(jnp.int32)
    counts = lax.optimization_barrier(jnp.sum(onehot * kept[..., None].astype(jnp.int32), axis=(0, 1, 2)))
    selector = (chosen.reshape(LEN * BATCH)[:, None] == jnp.arange(EXPERTS, dtype=jnp.int32)[None, :]).astype(jnp.float32)
    labels_by_sequence = document.T

    def forward(inputs, gain_one, shift_one, weight_in, weight_out, gain_two, shift_two, weight_up, weight_down, weight_router, weight_mixer, bias_mixer, experts_up, experts_down):
        flat = inputs.reshape(LEN * BATCH, D)
        normed_one = low(normalize(flat, gain_one, shift_one))
        projected = low(low_back(product(normed_one, weight_in)))
        by_sequence = projected.reshape(LEN, BATCH, 3 * D).transpose(1, 0, 2)
        attended = lax.map(lambda pair: attend_sequence(pair[0], pair[1]), (by_sequence, labels_by_sequence))
        attended = low(low_back(attended.transpose(1, 0, 2).reshape(LEN * BATCH, D)))
        hidden = flat + low_back(product(attended, weight_out))
        normed_two = low(normalize(hidden, gain_two, shift_two))
        dense_pre = low_back(product(normed_two, weight_up))
        dense_res = low_back(product(low(smooth(dense_pre)), weight_down))
        gates = jax.nn.softmax(product(normed_two, weight_router), axis=-1)
        chosen_gate = lax.optimization_barrier(jnp.sum(gates * selector, axis=-1, keepdims=True))
        mixing = jax.nn.softmax(product(normed_two, weight_mixer) + bias_mixer, axis=-1)
        buffer = jnp.zeros((slot_total + 1, D), jnp.float32).at[place].set(normed_two)
        buffer = low_back(buffer[:slot_total].reshape(EXPERTS, device_total * CAP, D))
        expert_pre = low_back(jnp.einsum('esd,def->esf', buffer, experts_up, precision=highest))
        produced = jnp.einsum('esf,fed->esd', low(smooth(expert_pre)), experts_down, precision=highest)
        produced = low(low_back(produced)).reshape(slot_total, D)
        produced = jnp.concatenate([produced, jnp.zeros((1, D), jnp.float32)], axis=0)
        combined = produced[place]
        output = hidden + mixing[:, :1] * dense_res + mixing[:, 1:] * (chosen_gate * combined)
        return output.reshape(LEN, BATCH, D)
    output, backward = jax.vjp(forward, tokens.astype(jnp.float32), first_gain, first_shift, project_in.astype(jnp.float32), project_out.astype(jnp.float32), second_gain, second_shift, dense_up.astype(jnp.float32), dense_down.astype(jnp.float32), router.astype(jnp.float32), mixer.astype(jnp.float32), mixer_bias, expert_up.astype(jnp.float32), expert_down.astype(jnp.float32))
    grads = backward(cotangent.astype(jnp.float32))
    load_after = momentum * load_before + (1.0 - momentum) * (counts.astype(jnp.float32) * EXPERTS / TOKENS)
    return (output.astype(jnp.bfloat16), grads[0].astype(jnp.bfloat16), grads[1], grads[2], grads[3], grads[4], grads[5], grads[6], grads[7], grads[8], grads[9], grads[10], grads[11], grads[12], grads[13], load_after)
```

```python
import functools

import jax
import jax.numpy as jnp
from jax import lax
from jax.experimental import pallas as pl
from jax.experimental.pallas import tpu as pltpu
from jax.sharding import Mesh, PartitionSpec as P

HEADS = 16
HEAD_DIM = 64
WIDE = ("chip", "core")
ALL = ("chip", "core", "narrow")

score_scale = 0.125
norm_eps = 1e-05
momentum = 0.3
masked_score = -1e30
gelu_slope = 0.7978845608028654
gelu_cubic = 0.044715

f32 = jnp.float32
bf16 = jnp.bfloat16


def mm(left, right, dims=((1,), (0,))):
    return lax.dot_general(left, right, (dims, ((), ())), preferred_element_type=f32)


def norm_stats(rows):
    average = jnp.mean(rows, axis=-1, keepdims=True)
    centered = rows - average
    variance = jnp.mean(centered * centered, axis=-1, keepdims=True)
    rstd = lax.rsqrt(variance + norm_eps)
    return centered * rstd, rstd


def norm_back(grad, gain, normed, rstd):
    scaled = grad * gain
    mean_scaled = jnp.mean(scaled, axis=-1, keepdims=True)
    mean_product = jnp.mean(scaled * normed, axis=-1, keepdims=True)
    return rstd * (scaled - mean_scaled - normed * mean_product)


def gelu_pair(u):
    square = u * u
    t = jnp.tanh(gelu_slope * u * (1.0 + gelu_cubic * square))
    half = 0.5 * (1.0 + t)
    slope = half + 0.5 * u * (1.0 - t * t) * (gelu_slope * (1.0 + 3.0 * gelu_cubic * square))
    return u * half, slope


def three_parts(value):
    high = lax.reduce_precision(value, 8, 7)
    rest = value - high
    middle = lax.reduce_precision(rest, 8, 7)
    low = lax.reduce_precision(rest - middle, 8, 7)
    return high, middle, low


def span_columns(ref, first, block, per):
    return jnp.concatenate(
        [ref[block * per + t, first : first + HEAD_DIM, :] for t in range(per)], axis=1
    )


def rows_of(columns):
    return jnp.transpose(columns.astype(f32)).astype(bf16)


def iotas(span):
    shape = (span, span)
    return (
        lax.broadcasted_iota(jnp.int32, shape, 0),
        lax.broadcasted_iota(jnp.int32, shape, 1),
    )


def fold_rows(tile, op):
    return op(tile.reshape(tile.shape[0] // 8, 8, tile.shape[1]), axis=0)


def label_row(ref, block, per):
    return jnp.concatenate(
        [ref[block * per + t, 192:208, :].astype(f32)[0:1] for t in range(per)], axis=1
    )


def attend_kernel(span, per, qkv_ref, low_ref, wide_ref, lse_ref, key_s, label_s, score_s):
    blocks, _, rows = qkv_ref.shape
    count = blocks // per

    @pl.loop(0, blocks)
    def _(j):
        at = pl.ds(pl.multiple_of(j * rows, rows), rows)
        key_s[at, :] = rows_of(qkv_ref[j, 64:128, :])
        label_s[at, :] = jnp.transpose(qkv_ref[j, 192:208, :].astype(f32))

    row_at, column_at = iotas(span)

    @pl.loop(0, count)
    def _(i):
        query = (span_columns(qkv_ref, 0, i, per).astype(f32) * score_scale).astype(bf16)
        labels = label_row(qkv_ref, i, per)

        def score(j, peak):
            at = pl.ds(pl.multiple_of(j * span, span), span)
            s = mm(key_s[at, :], query)
            keep = (label_s[at, 0:1] == labels) & (j * span + row_at <= i * span + column_at)
            s = jnp.where(keep, s, masked_score)
            score_s[at, :] = s
            return jnp.maximum(peak, fold_rows(s, jnp.max))

        peak = lax.fori_loop(0, i + 1, score, jnp.full((8, span), masked_score, f32))
        peak = jnp.max(peak, axis=0, keepdims=True)

        def weigh(j, total):
            at = pl.ds(pl.multiple_of(j * span, span), span)
            e = jnp.exp(score_s[at, :] - peak)
            score_s[at, :] = e
            return total + fold_rows(e, jnp.sum)

        total = lax.fori_loop(0, i + 1, weigh, jnp.zeros((8, span), f32))
        total = jnp.sum(total, axis=0, keepdims=True)
        share = 1.0 / total

        def mix(j, out):
            at = pl.ds(pl.multiple_of(j * span, span), span)
            p = (score_s[at, :] * share).astype(bf16)
            return out + mm(span_columns(qkv_ref, 128, j, per), p)

        out = lax.fori_loop(0, i + 1, mix, jnp.zeros((HEAD_DIM, span), f32))
        for t in range(per):
            part = out[:, t * rows : (t + 1) * rows]
            wide_ref[i * per + t] = part
            low_ref[i * per + t] = part.astype(bf16)
        lse_ref[i] = peak + jnp.log(total)


def attend_back_kernel(
    span, per, qkv_ref, do_ref, wide_ref, lse_ref, out_ref, flat_ref,
    query_s, key_s, value_s, grad_s, label_s, delta_s, dq_s,
):
    blocks, _, rows = qkv_ref.shape
    count = blocks // per

    @pl.loop(0, blocks)
    def _(j):
        at = pl.ds(pl.multiple_of(j * rows, rows), rows)
        query_s[at, :] = rows_of(qkv_ref[j, 0:64, :])
        key_s[at, :] = rows_of(qkv_ref[j, 64:128, :])
        value_s[at, :] = rows_of(qkv_ref[j, 128:192, :])
        grad_s[at, :] = rows_of(do_ref[j])
        label_s[at, :] = jnp.transpose(qkv_ref[j, 192:208, :].astype(f32))
        delta_s[j] = jnp.sum(do_ref[j].astype(f32) * wide_ref[j], axis=0, keepdims=True)

    dq_s[...] = jnp.zeros_like(dq_s)
    row_at, column_at = iotas(span)

    @pl.loop(0, count)
    def _(j):
        at = pl.ds(pl.multiple_of(j * span, span), span)
        keys, values = key_s[at, :], value_s[at, :]
        key_columns = span_columns(qkv_ref, 64, j, per)
        key_labels = label_s[at, 0:1]

        def step(i, carry):
            dk, dv = carry
            to = pl.ds(pl.multiple_of(i * span, span), span)
            query = (span_columns(qkv_ref, 0, i, per).astype(f32) * score_scale).astype(bf16)
            grad = jnp.concatenate([do_ref[i * per + t] for t in range(per)], axis=1)
            delta = jnp.concatenate([delta_s[i * per + t] for t in range(per)], axis=1)
            labels = label_row(qkv_ref, i, per)
            s = mm(keys, query)
            keep = (key_labels == labels) & (j * span + row_at <= i * span + column_at)
            p = jnp.where(keep, jnp.exp(s - lse_ref[i]), 0.0)
            dp = mm(values, grad)
            ds = (p * (dp - delta)).astype(bf16)
            dq_s[i] = dq_s[i] + mm(key_columns, ds)
            dk = dk + mm(ds, query_s[to, :])
            dv = dv + mm(p.astype(bf16), grad_s[to, :])
            return dk, dv

        zero = jnp.zeros((span, HEAD_DIM), f32)
        dk, dv = lax.fori_loop(j, count, step, (zero, zero))
        dk = jnp.transpose(dk * score_scale).astype(bf16)
        dv = jnp.transpose(dv).astype(bf16)
        flat_ref[64:128, at] = dk
        flat_ref[128:192, at] = dv
        for t in range(per):
            part = slice(t * rows, (t + 1) * rows)
            out_ref[j * per + t, 64:128, :] = dk[:, part]
            out_ref[j * per + t, 128:192, :] = dv[:, part]

    @pl.loop(0, count)
    def _(i):
        at = pl.ds(pl.multiple_of(i * span, span), span)
        dq = (dq_s[i] * score_scale).astype(bf16)
        flat_ref[0:64, at] = dq
        for t in range(per):
            out_ref[i * per + t, 0:64, :] = dq[:, t * rows : (t + 1) * rows]


def attend(qkv):
    blocks, _, rows = qkv.shape
    per = max(1, 256 // rows)
    span, length = per * rows, blocks * rows
    return pl.pallas_call(
        functools.partial(attend_kernel, span, per),
        out_shape=(
            jax.ShapeDtypeStruct((blocks, HEAD_DIM, rows), bf16),
            jax.ShapeDtypeStruct((blocks, HEAD_DIM, rows), f32),
            jax.ShapeDtypeStruct((length // span, 1, span), f32),
        ),
        scratch_shapes=[
            pltpu.VMEM((length, HEAD_DIM), bf16),
            pltpu.VMEM((length, 16), f32),
            pltpu.VMEM((length, span), f32),
        ],
        compiler_params=pltpu.CompilerParams(vmem_limit_bytes=24 * 2**20),
        cost_estimate=pl.CostEstimate(
            flops=length * length * HEAD_DIM * 2,
            bytes_accessed=length * 1024,
            transcendentals=length * length // 2,
        ),
        name="attend",
    )(qkv)


def attend_back(qkv, grad, wide, lse):
    blocks, _, rows = qkv.shape
    per = max(1, 256 // rows)
    span, length = per * rows, blocks * rows
    return pl.pallas_call(
        functools.partial(attend_back_kernel, span, per),
        out_shape=(
            jax.ShapeDtypeStruct((blocks, 3 * HEAD_DIM, rows), bf16),
            jax.ShapeDtypeStruct((3 * HEAD_DIM, length), bf16),
        ),
        scratch_shapes=[
            pltpu.VMEM((length, HEAD_DIM), bf16),
            pltpu.VMEM((length, HEAD_DIM), bf16),
            pltpu.VMEM((length, HEAD_DIM), bf16),
            pltpu.VMEM((length, HEAD_DIM), bf16),
            pltpu.VMEM((length, 16), f32),
            pltpu.VMEM((blocks, 1, rows), f32),
            pltpu.VMEM((length // span, HEAD_DIM, span), f32),
        ],
        compiler_params=pltpu.CompilerParams(vmem_limit_bytes=32 * 2**20),
        cost_estimate=pl.CostEstimate(
            flops=length * length * HEAD_DIM * 5,
            bytes_accessed=length * 2048,
            transcendentals=length * length // 2,
        ),
        name="attend_back",
    )(qkv, grad, wide, lse)


def feed_kernel(rows_ref, grad_ref, up_ref, down_ref, out_ref, back_ref):
    step = pl.program_id(0)
    up, down = up_ref[...], down_ref[...]
    act, slope = gelu_pair(mm(rows_ref[...], up))
    out = mm(act.astype(bf16), down)
    inner = (mm(grad_ref[...], down, ((1,), (1,))) * slope).astype(bf16)
    back = mm(inner, up, ((1,), (1,)))

    @pl.when(step == 0)
    def _():
        out_ref[...] = out
        back_ref[...] = back

    @pl.when(step > 0)
    def _():
        out_ref[...] += out
        back_ref[...] += back


def feed(rows, grad, up, down):
    count, width = rows.shape
    hidden = up.shape[1]
    chunk = min(hidden, 512)
    whole = pl.BlockSpec((count, width), lambda c: (0, 0))
    return pl.pallas_call(
        feed_kernel,
        grid=(hidden // chunk,),
        in_specs=[
            whole,
            whole,
            pl.BlockSpec((width, chunk), lambda c: (0, c)),
            pl.BlockSpec((chunk, width), lambda c: (c, 0)),
        ],
        out_specs=[whole, whole],
        out_shape=[jax.ShapeDtypeStruct((count, width), f32)] * 2,
        compiler_params=pltpu.CompilerParams(vmem_limit_bytes=24 * 2**20),
        cost_estimate=pl.CostEstimate(
            flops=8 * count * width * hidden,
            bytes_accessed=4 * width * hidden,
            transcendentals=count * hidden,
        ),
        name="feed",
    )(rows, grad, up, down)


def slice_kernel(
    steps, expert_units, mine_ref, rows_ref, grad_ref, up_ref, down_ref, up_out, down_out, up_acc, down_acc
):
    step = pl.program_id(0)
    count = grad_ref.shape[1]

    @pl.when(step == 0)
    def _():
        up_acc[...] = jnp.zeros_like(up_acc)
        down_acc[...] = jnp.zeros_like(down_acc)

    rows, dense_grad, expert_grad = [], [], []
    for t in range(rows_ref.shape[0]):
        scalars = jnp.transpose(rows_ref[t, count : count + 8, 0:count].astype(f32))
        mixing = scalars[:, 0:1] + scalars[:, 1:2] + scalars[:, 2:3]
        gate = scalars[:, 3:4] + scalars[:, 4:5] + scalars[:, 5:6]
        mine = scalars[:, 6:7] == mine_ref[0].astype(f32)
        grad = grad_ref[t].astype(f32)
        rows.append(rows_ref[t, 0:count, :])
        dense_grad.append((mixing * grad).astype(bf16))
        expert_grad.append((jnp.where(mine, gate, 0.0) * grad).astype(bf16))
    rows = jnp.concatenate(rows, axis=0)
    dense_grad = jnp.concatenate(dense_grad, axis=0)
    expert_grad = jnp.concatenate(expert_grad, axis=0)
    act, slope = gelu_pair(mm(rows, up_ref[...]))
    act = act.astype(bf16)
    inner = jnp.concatenate(
        [mm(expert_grad, down_ref[:, :expert_units]), mm(dense_grad, down_ref[:, expert_units:])],
        axis=1,
    )
    inner = (inner * slope).astype(bf16)
    first = ((0,), (0,))
    up_acc[...] += mm(inner, rows, first)
    down_acc[:expert_units, :] += mm(act[:, :expert_units], expert_grad, first)
    down_acc[expert_units:, :] += mm(act[:, expert_units:], dense_grad, first)

    @pl.when(step == steps - 1)
    def _():
        up_out[...] = jnp.transpose(up_acc[...]).astype(bf16)
        down_out[...] = down_acc[...]


def slice_grads(mine, rows, grad, up, down, expert_units):
    devices, padded, width = rows.shape
    count = grad.shape[1]
    units = up.shape[1]
    per = 2
    steps = devices // per
    fixed = pl.BlockSpec((width, units), lambda c, m: (0, 0))
    return pl.pallas_call(
        functools.partial(slice_kernel, steps, expert_units),
        grid_spec=pltpu.PrefetchScalarGridSpec(
            num_scalar_prefetch=1,
            grid=(steps,),
            in_specs=[
                pl.BlockSpec((per, padded, width), lambda c, m: (c, 0, 0)),
                pl.BlockSpec((per, count, width), lambda c, m: (c, 0, 0)),
                fixed,
                fixed,
            ],
            out_specs=[
                pl.BlockSpec((width, units), lambda c, m: (0, 0)),
                pl.BlockSpec((units, width), lambda c, m: (0, 0)),
            ],
            scratch_shapes=[pltpu.VMEM((units, width), f32), pltpu.VMEM((units, width), f32)],
        ),
        out_shape=[
            jax.ShapeDtypeStruct((width, units), bf16),
            jax.ShapeDtypeStruct((units, width), f32),
        ],
        compiler_params=pltpu.CompilerParams(vmem_limit_bytes=32 * 2**20),
        cost_estimate=pl.CostEstimate(
            flops=8 * devices * count * width * units,
            bytes_accessed=4 * devices * count * width,
            transcendentals=devices * count * units,
        ),
        name="slice_grads",
    )(mine, rows, grad, up, down)


def gather(value):
    return lax.all_gather(value, WIDE, axis=0, tiled=True)


def exchange(columns):
    wide = lax.axis_size("chip") * lax.axis_size("core")
    blocks = columns.astype(bf16).reshape(wide, columns.shape[0] // wide, columns.shape[1])
    got = lax.all_to_all(blocks, WIDE, 0, 0, tiled=True)
    return got.transpose(1, 0, 2).reshape(blocks.shape[1], wide * blocks.shape[2])


def plain_slice(rows, grad, up, down):
    act, slope = gelu_pair(mm(rows, up))
    inner = (mm(grad, down, ((1,), (1,))) * slope).astype(bf16)
    return mm(rows, inner, ((0,), (0,))), mm(act.astype(bf16), grad, ((0,), (0,)))


def other_narrow(value):
    size = lax.axis_size("narrow")
    if size != 2:
        return lax.all_gather(value, "narrow", axis=0, tiled=False)
    swapped = lax.ppermute(value, "narrow", [(0, 1), (1, 0)])
    first = lax.axis_index("narrow") == 0
    return jnp.stack([jnp.where(first, value, swapped), jnp.where(first, swapped, value)])


def local(
    tokens, document, routing, capacity, load_before, first_gain, first_shift, project_in,
    project_out, second_gain, second_shift, dense_up, dense_down, router, mixer, mixer_bias,
    expert_up, expert_down, cotangent,
):
    rows, seq_count, width = tokens.shape
    assert seq_count == 1 and width == HEADS * HEAD_DIM
    wide, narrow = lax.axis_size("chip") * lax.axis_size("core"), lax.axis_size("narrow")
    devices = wide * narrow
    experts = capacity.shape[0]
    hidden_units = dense_up.shape[1]
    assert experts == narrow and wide % HEADS == 0
    copies = wide // HEADS
    my_wide = lax.axis_index("chip") * lax.axis_size("core") + lax.axis_index("core")
    my_narrow = lax.axis_index("narrow")

    inputs = tokens.reshape(rows, width).astype(f32)
    grad_low = cotangent.reshape(rows, width)
    grad_out = grad_low.astype(f32)
    gather_all = devices * rows * width <= 2**23
    if gather_all:
        grad_all = lax.all_gather(grad_low, ALL, axis=0, tiled=False)

    normed_one, rstd_one = norm_stats(inputs)
    a = (normed_one * first_gain + first_shift).astype(bf16)
    projected = mm(a, project_in).astype(bf16)
    a_all = lax.all_gather(a, WIDE, axis=0, tiled=True)
    by_head = projected.reshape(rows, 3, HEADS, HEAD_DIM).transpose(2, 1, 3, 0)
    by_head = by_head.reshape(HEADS, 3 * HEAD_DIM, rows)
    labels = jnp.broadcast_to(document.reshape(1, 1, rows).astype(bf16), (HEADS, 16, rows))
    payload = jnp.concatenate([by_head, labels], axis=1)
    payload = jnp.repeat(payload, copies, axis=0)
    qkv = lax.all_to_all(payload, WIDE, 0, 0, tiled=True)
    head_low, head_wide, lse = attend(qkv)
    attended = lax.all_to_all(head_low, WIDE, 0, 0, tiled=True)[::copies].reshape(width, rows)

    hidden = inputs + mm(attended, project_out, ((0,), (0,)))
    normed_two, rstd_two = norm_stats(hidden)
    b = (normed_two * second_gain + second_shift).astype(bf16)

    def scores_of(values):
        gates = jax.nn.softmax(mm(values, router), axis=-1)
        mixing = jax.nn.softmax(mm(values, mixer) + mixer_bias, axis=-1)
        return gates, mixing

    gates, mixing = scores_of(b)
    chosen = routing.reshape(rows)
    onehot = (chosen[:, None] == jnp.arange(experts, dtype=jnp.int32)[None, :]).astype(jnp.int32)
    chosen_gate = jnp.sum(gates * onehot, axis=-1, keepdims=True)
    earlier = jnp.cumsum(onehot, axis=0) - onehot
    slot_rank = jnp.sum(earlier * onehot, axis=-1)
    kept = slot_rank < jnp.sum(capacity[None, :] * onehot, axis=-1)
    counts = jnp.sum(onehot * kept[:, None].astype(jnp.int32), axis=0)
    slots = rows * 5 // (4 * experts)
    slot_index = chosen * slots + slot_rank
    dispatch = (
        (slot_index[None, :] == jnp.arange(experts * slots, dtype=jnp.int32)[:, None])
        & kept[None, :]
    ).astype(bf16)

    def send_slots(values):
        filled = mm(dispatch, values).astype(bf16).reshape(experts, slots, width)
        return lax.all_to_all(filled, "narrow", 0, 0, tiled=True).reshape(narrow * slots, width)

    slot_grad = send_slots(grad_low)
    slot_rows = send_slots(b)

    own = width // wide
    code = jnp.where(kept, chosen, experts).astype(f32)
    scalars = jnp.stack(
        [*three_parts(mixing[:, 0]), *three_parts(mixing[:, 1] * chosen_gate[:, 0]), code, code]
    )
    scalars = jnp.pad(scalars.astype(bf16), ((0, 0), (0, width - rows)))
    if gather_all:
        rows_all = lax.all_gather(jnp.concatenate([b, scalars]), ALL, axis=0, tiled=False)

    dense_grad = (mixing[:, :1] * grad_out).astype(bf16)
    dense_res, dense_back = feed(b, dense_grad, dense_up, dense_down)

    my_up = expert_up.reshape(width, hidden_units)
    my_down = expert_down.reshape(hidden_units, width)
    slot_gates, slot_mixing = scores_of(slot_rows)
    slot_gate = lax.dynamic_index_in_dim(slot_gates, my_narrow, axis=1)
    slot_back = (slot_gate * (slot_mixing[:, 1:] * slot_grad.astype(f32))).astype(bf16)
    slot_out, slot_rows_grad = feed(slot_rows, slot_back, my_up, my_down)
    results = jnp.concatenate(
        [
            slot_out.astype(bf16).reshape(narrow, slots, width),
            slot_rows_grad.astype(bf16).reshape(narrow, slots, width),
        ],
        axis=1,
    )
    returned = lax.all_to_all(results, "narrow", 0, 0, tiled=True)

    def from_slots(values):
        return mm(dispatch, values.reshape(experts * slots, width), ((0,), (0,)))

    expert_raw = from_slots(returned[:, :slots])
    expert_back = from_slots(returned[:, slots:])
    expert_res = chosen_gate * expert_raw
    output = hidden + mixing[:, :1] * dense_res + mixing[:, 1:] * expert_res
    result = output.astype(bf16).reshape(rows, 1, width)

    grad_gate = jnp.sum(mixing[:, 1:] * grad_out * expert_raw, axis=-1, keepdims=True)
    grad_mixing = jnp.concatenate(
        [
            jnp.sum(grad_out * dense_res, axis=-1, keepdims=True),
            jnp.sum(grad_out * expert_res, axis=-1, keepdims=True),
        ],
        axis=-1,
    )
    grad_mix_logits = mixing * (grad_mixing - jnp.sum(mixing * grad_mixing, axis=-1, keepdims=True))
    grad_router_logits = gates * (onehot.astype(f32) - chosen_gate) * grad_gate
    grad_b = dense_back + expert_back
    for e in range(experts):
        grad_b = grad_b + grad_router_logits[:, e : e + 1] * router[:, e].astype(f32)[None, :]
    for e in range(2):
        grad_b = grad_b + grad_mix_logits[:, e : e + 1] * mixer[:, e].astype(f32)[None, :]
    logit_grads = jnp.concatenate([grad_router_logits, grad_mix_logits], axis=1)
    small_part = jnp.einsum(
        "nd,ne->de", b.astype(f32), logit_grads, precision=lax.Precision.HIGHEST
    )
    second_gain_part = jnp.sum(grad_b * normed_two, axis=0)
    second_shift_part = jnp.sum(grad_b, axis=0)
    grad_hidden = grad_out + norm_back(grad_b, second_gain, normed_two, rstd_two)
    grad_attn = grad_hidden.astype(bf16)

    grad_heads = mm(project_out, grad_attn, ((1,), (1,))).astype(bf16)
    grad_heads = grad_heads.reshape(HEADS, HEAD_DIM, rows)
    grad_heads = jnp.repeat(grad_heads, copies, axis=0)
    head_grad = lax.all_to_all(grad_heads, WIDE, 0, 0, tiled=True)
    grad_blocks, grad_flat = attend_back(qkv, head_grad, head_wide, lse)
    sent_back = lax.all_to_all(grad_blocks, WIDE, 0, 0, tiled=True)[::copies]
    grad_qkv = sent_back.reshape(HEADS, 3, HEAD_DIM, rows).transpose(1, 0, 2, 3)
    grad_qkv = grad_qkv.reshape(3 * width, rows)
    grad_a = mm(grad_qkv, project_in, ((0,), (1,)))
    first_gain_part = jnp.sum(grad_a * normed_one, axis=0)
    first_shift_part = jnp.sum(grad_a, axis=0)
    input_grad = grad_hidden + norm_back(grad_a, first_gain, normed_one, rstd_one)
    input_grad = input_grad.astype(bf16).reshape(rows, 1, width)

    chips, cores = lax.axis_size("chip"), lax.axis_size("core")
    assert cores == 2
    core = lax.axis_index("core")
    out_part = mm(attended, grad_attn).reshape(chips, cores, own, width)
    swap = [(0, 1), (1, 0)]
    mine = lax.dynamic_index_in_dim(out_part, core, axis=1, keepdims=False)
    theirs = lax.dynamic_index_in_dim(out_part, 1 - core, axis=1, keepdims=False)
    out_pair = mine + lax.ppermute(theirs.astype(bf16), "core", swap).astype(f32)
    out_blocks = lax.all_to_all(out_pair.astype(bf16), "chip", 0, 0, tiled=True)
    out_sum = jnp.sum(out_blocks.astype(f32), axis=0)
    project_out_grad = jnp.sum(other_narrow(out_sum.astype(bf16)).astype(f32), axis=0)

    expert_units, dense_units = hidden_units // wide, hidden_units // devices
    up_slice = lax.dynamic_slice_in_dim(my_up, my_wide * expert_units, expert_units, axis=1)
    down_slice = lax.dynamic_slice_in_dim(my_down, my_wide * expert_units, expert_units, axis=0)
    if gather_all:
        lanes = -(-dense_units // 128) * 128
        dense_first = my_wide * expert_units + my_narrow * dense_units
        dense_up_slice = lax.dynamic_slice_in_dim(dense_up, dense_first, dense_units, axis=1)
        dense_down_slice = lax.dynamic_slice_in_dim(dense_down, dense_first, dense_units, axis=0)
        fill = ((0, 0), (0, lanes - dense_units))
        ups = jnp.concatenate([up_slice, jnp.pad(dense_up_slice, fill)], axis=1)
        downs = jnp.concatenate([down_slice.T, jnp.pad(dense_down_slice.T, fill)], axis=1)
        ups_part, downs_part = slice_grads(
            my_narrow.astype(jnp.int32).reshape(1), rows_all, grad_all, ups, downs, expert_units
        )
        expert_down_grad = downs_part[:expert_units].reshape(expert_units, 1, width)
        dense_down_part = downs_part[expert_units : expert_units + dense_units].astype(bf16)
        dense_down_grad = other_narrow(dense_down_part).astype(f32)
        dense_down_grad = dense_down_grad.reshape(narrow * dense_units, width)
        ups_blocks = ups_part[:, : expert_units + dense_units].reshape(wide, own, -1)
        ups_got = lax.all_to_all(ups_blocks, WIDE, 0, 0, tiled=True)
        expert_up_grad = ups_got[:, :, :expert_units].transpose(1, 0, 2).astype(f32)
        expert_up_grad = expert_up_grad.reshape(own, 1, hidden_units)
        dense_got = other_narrow(ups_got[:, :, expert_units:])
        dense_up_grad = dense_got.transpose(2, 1, 0, 3).reshape(own, hidden_units).astype(f32)
    else:
        dense_up_slice = lax.dynamic_slice_in_dim(
            dense_up, my_wide * expert_units, expert_units, axis=1
        )
        dense_down_slice = lax.dynamic_slice_in_dim(
            dense_down, my_wide * expert_units, expert_units, axis=0
        )
        dense_up_part, dense_down_part = plain_slice(
            gather(b), gather(dense_grad), dense_up_slice, dense_down_slice
        )
        dense_down_grad = lax.psum(dense_down_part.astype(bf16), "narrow").astype(f32)
        dense_up_grad = lax.psum(exchange(dense_up_part), "narrow").astype(f32)
        expert_up_part, expert_down_grad = plain_slice(
            gather(slot_rows), gather(slot_back), up_slice, down_slice
        )
        expert_down_grad = expert_down_grad.reshape(expert_units, 1, width)
        expert_up_grad = exchange(expert_up_part).astype(f32).reshape(own, 1, hidden_units)

    in_part = mm(grad_flat, a_all).astype(bf16)
    half = 3 * HEAD_DIM // 2
    in_blocks = in_part.reshape(2, half, wide, own).transpose(2, 1, 0, 3)
    in_blocks = in_blocks.reshape(wide, half * 2 * own // 128, 128)
    bias_parts = jnp.stack(three_parts(jnp.sum(grad_mix_logits, axis=0))).reshape(1, 6)
    vectors = jnp.stack([first_gain_part, first_shift_part, second_gain_part, second_shift_part])
    vectors = vectors.reshape(4, wide, own).transpose(1, 0, 2).reshape(wide, 4 * own)
    small = small_part.reshape(wide, own * (experts + 2))
    flat = jnp.concatenate([vectors, small, jnp.broadcast_to(bias_parts, (wide, 6))], axis=1)
    short = -(-flat.shape[1] // 2048) * 2048
    flat = jnp.pad(flat, ((0, 0), (0, short - flat.shape[1]))).astype(bf16)
    both = jnp.concatenate([in_blocks, flat.reshape(wide, short // 128, 128)], axis=1)
    both = jnp.broadcast_to(both[:, None], (wide, narrow) + both.shape[1:])
    both = both.reshape((devices,) + both.shape[2:])
    got = lax.all_to_all(both, ALL, 0, 0, tiled=True)
    got = got.reshape((wide, narrow) + got.shape[1:])
    in_rows = in_blocks.shape[1]
    in_sum = jnp.sum(got[::copies, :, :in_rows].astype(f32), axis=1)
    in_sum = in_sum.reshape(HEADS, half, 2, own).transpose(0, 2, 1, 3)
    in_sum = in_sum.reshape(HEADS, 3, HEAD_DIM, own).transpose(3, 1, 0, 2)
    project_in_grad = in_sum.reshape(own, 3 * width)
    sums = jnp.sum(got[:, :, in_rows:].astype(f32), axis=(0, 1)).reshape(short)
    vector_sums = sums[: 4 * own].reshape(4, own)
    small_sum = sums[4 * own : own * (6 + experts)].reshape(own, experts + 2)
    bias_at = own * (6 + experts)
    mixer_bias_grad = jnp.sum(sums[bias_at : bias_at + 6].reshape(3, 2), axis=0)

    if gather_all:
        codes = rows_all[:, rows + 6, :rows].astype(f32).reshape(devices * rows, 1)
        count_sum = jnp.sum((codes == jnp.arange(experts, dtype=f32)[None, :]).astype(f32), axis=0)
    else:
        count_sum = lax.psum(counts.astype(f32), ALL)
    load_after = momentum * load_before + (1.0 - momentum) * (
        count_sum * experts / (devices * rows)
    )
    return (
        result,
        input_grad,
        vector_sums[0],
        vector_sums[1],
        project_in_grad,
        project_out_grad,
        vector_sums[2],
        vector_sums[3],
        dense_up_grad,
        dense_down_grad,
        small_sum[:, :experts],
        small_sum[:, experts:],
        mixer_bias_grad,
        expert_up_grad,
        expert_down_grad,
        load_after,
    )


def solution(mesh):
    wide, narrow = mesh.devices.shape
    fine = Mesh(mesh.devices.reshape(wide // 2, 2, narrow), ALL)
    by_token = P(WIDE, "narrow", None)
    by_expert = P(None, "narrow", None)
    return jax.shard_map(
        local,
        mesh=fine,
        in_specs=(
            by_token, P(WIDE, "narrow"), by_token, P(), P(), P(), P(), P(), P(), P(), P(), P(),
            P(), P(), P(), P(), by_expert, by_expert, by_token,
        ),
        out_specs=(
            by_token, by_token, P(WIDE), P(WIDE), P(WIDE, None), P(WIDE, None), P(WIDE), P(WIDE),
            P(WIDE, None), P(WIDE, None), P(WIDE, None), P(WIDE, None), P(), by_token, by_token,
            P(),
        ),
        check_vma=False,
    )
```

```python
import functools

import jax
import jax.numpy as jnp
from jax import lax
from jax.experimental import pallas as pl
from jax.experimental.pallas import tpu as pltpu
from jax.sharding import Mesh, PartitionSpec as P

HEADS = 16
HEAD_DIM = 64
WIDE = ("chip", "core")
ALL = ("chip", "core", "narrow")

score_scale = 0.125
norm_eps = 1e-05
momentum = 0.3
masked_score = -1e30
gelu_slope = 0.7978845608028654
gelu_cubic = 0.044715

f32 = jnp.float32
bf16 = jnp.bfloat16


def mm(left, right, dims=((1,), (0,))):
    return lax.dot_general(left, right, (dims, ((), ())), preferred_element_type=f32)


def norm_stats(rows):
    average = jnp.mean(rows, axis=-1, keepdims=True)
    centered = rows - average
    variance = jnp.mean(centered * centered, axis=-1, keepdims=True)
    rstd = lax.rsqrt(variance + norm_eps)
    return centered * rstd, rstd


def norm_back(grad, gain, normed, rstd):
    scaled = grad * gain
    mean_scaled = jnp.mean(scaled, axis=-1, keepdims=True)
    mean_product = jnp.mean(scaled * normed, axis=-1, keepdims=True)
    return rstd * (scaled - mean_scaled - normed * mean_product)


def gelu_pair(u):
    square = u * u
    t = jnp.tanh(gelu_slope * u * (1.0 + gelu_cubic * square))
    half = 0.5 * (1.0 + t)
    slope = half + 0.5 * u * (1.0 - t * t) * (gelu_slope * (1.0 + 3.0 * gelu_cubic * square))
    return u * half, slope


def three_parts(value):
    high = lax.reduce_precision(value, 8, 7)
    rest = value - high
    middle = lax.reduce_precision(rest, 8, 7)
    low = lax.reduce_precision(rest - middle, 8, 7)
    return high, middle, low


SPAN = 256
TILE = 256


def columns(ref, first, block, per):
    return jnp.concatenate(
        [ref[block * per + t, first : first + HEAD_DIM, :] for t in range(per)], axis=1
    )


def rows_of(values):
    return jnp.transpose(values.astype(f32)).astype(bf16)


def fold(tile, op):
    return op(tile.reshape(tile.shape[0] // 8, 8, tile.shape[1]), axis=0)


def repeat(low, high, body, carry, unrolled):
    if unrolled:
        for step in range(low, high):
            carry = body(step, carry)
        return carry
    return lax.fori_loop(low, high, body, carry)


def aligned(index, size):
    start = index * size
    return pl.ds(start if isinstance(index, int) else pl.multiple_of(start, size), size)


def document_starts(qkv_ref, start_s):
    labels = [qkv_ref[j, 192:208, :].astype(f32)[0:1] for j in range(qkv_ref.shape[0])]
    every = jnp.concatenate(labels, axis=0)
    counts = [jnp.sum((every < v).astype(f32), keepdims=True) for v in range(1, 5)]
    before = [jnp.zeros_like(counts[0])] + counts[:-1]
    start = sum(
        jnp.where(every >= v + 1, counts[v] - before[v], 0.0) for v in range(4)
    ).astype(jnp.int32)
    for j in range(qkv_ref.shape[0]):
        start_s[j] = start[j : j + 1]


def allowed(first_key, start, first_query, row_at, column_at, diagonal):
    keep = row_at >= start - first_key
    if diagonal is None or diagonal:
        keep = keep & (row_at - column_at <= first_query - first_key)
    return keep


def attend_kernel(unrolled, qkv_ref, low_ref, wide_ref, lse_ref, key_s, start_s, score_s):
    blocks, _, rows = qkv_ref.shape
    per = SPAN // rows
    count, ratio = blocks // per, SPAN // TILE
    for j in range(blocks):
        key_s[j * rows : (j + 1) * rows, :] = rows_of(qkv_ref[j, 64:128, :])
    document_starts(qkv_ref, start_s)
    shape = (TILE, SPAN)
    row_at = lax.broadcasted_iota(jnp.int32, shape, 0)
    column_at = lax.broadcasted_iota(jnp.int32, shape, 1)

    def block(i, _):
        query = (columns(qkv_ref, 0, i, per).astype(f32) * score_scale).astype(bf16)
        start = jnp.concatenate([start_s[i * per + t] for t in range(per)], axis=1)
        slot = i % 2

        def score(j, peak):
            at = aligned(j, TILE)
            s = mm(key_s[at, :], query)
            diagonal = j >= i * ratio if unrolled else None
            keep = allowed(j * TILE, start, i * SPAN, row_at, column_at, diagonal)
            s = jnp.where(keep, s, masked_score)
            score_s[slot, at, :] = s
            return jnp.maximum(peak, fold(s, jnp.max))

        end = (i + 1) * ratio
        peak = repeat(0, end, score, jnp.full((8, SPAN), masked_score, f32), unrolled)
        peak = jnp.max(peak, axis=0, keepdims=True)

        def weigh(j, total):
            at = aligned(j, TILE)
            e = jnp.exp(score_s[slot, at, :] - peak)
            score_s[slot, at, :] = e
            return total + fold(e, jnp.sum)

        total = repeat(0, end, weigh, jnp.zeros((8, SPAN), f32), unrolled)
        total = jnp.sum(total, axis=0, keepdims=True)
        share = 1.0 / total

        def mix(j, out):
            p = (score_s[slot, aligned(j, SPAN), :] * share).astype(bf16)
            return out + mm(columns(qkv_ref, 128, j, per), p)

        out = repeat(0, i + 1, mix, jnp.zeros((HEAD_DIM, SPAN), f32), unrolled)
        for t in range(per):
            part = out[:, t * rows : (t + 1) * rows]
            wide_ref[i * per + t] = part
            low_ref[i * per + t] = part.astype(bf16)
        lse_ref[i] = peak + jnp.log(total)
        return 0

    repeat(0, count, block, 0, unrolled)


def attend_back_kernel(
    unrolled, qkv_ref, do_ref, wide_ref, lse_ref, out_ref,
    query_s, key_s, value_s, grad_s, start_s, delta_s, dk_s, dv_s, ds_s,
):
    blocks, _, rows = qkv_ref.shape
    per = SPAN // rows
    count, ratio = blocks // per, SPAN // TILE
    for j in range(blocks):
        at = slice(j * rows, (j + 1) * rows)
        query_s[at, :] = rows_of(qkv_ref[j, 0:64, :])
        key_s[at, :] = rows_of(qkv_ref[j, 64:128, :])
        value_s[at, :] = rows_of(qkv_ref[j, 128:192, :])
        grad_s[at, :] = rows_of(do_ref[j])
        delta_s[j] = jnp.sum(do_ref[j].astype(f32) * wide_ref[j], axis=0, keepdims=True)
    document_starts(qkv_ref, start_s)
    shape = (TILE, SPAN)
    row_at = lax.broadcasted_iota(jnp.int32, shape, 0)
    column_at = lax.broadcasted_iota(jnp.int32, shape, 1)
    if not unrolled:
        dk_s[...] = jnp.zeros_like(dk_s)
        dv_s[...] = jnp.zeros_like(dv_s)

    def block(i, _):
        query = (columns(qkv_ref, 0, i, per).astype(f32) * score_scale).astype(bf16)
        grad = jnp.concatenate([do_ref[i * per + t] for t in range(per)], axis=1)
        start = jnp.concatenate([start_s[i * per + t] for t in range(per)], axis=1)
        delta = jnp.concatenate([delta_s[i * per + t] for t in range(per)], axis=1)
        lse = lse_ref[i]
        query_rows, grad_rows = query_s[aligned(i, SPAN), :], grad_s[aligned(i, SPAN), :]
        slot = i % 2

        def tile(j, dq):
            at = aligned(j, TILE)
            s = mm(key_s[at, :], query)
            diagonal = j >= i * ratio if unrolled else None
            keep = allowed(j * TILE, start, i * SPAN, row_at, column_at, diagonal)
            p = jnp.where(keep, jnp.exp(s - lse), 0.0)
            ds = (p * (mm(value_s[at, :], grad) - delta)).astype(bf16)
            p = p.astype(bf16)
            dk, dv = mm(ds, query_rows), mm(p, grad_rows)
            if unrolled and diagonal:
                dk_s[at, :] = dk
                dv_s[at, :] = dv
            else:
                dk_s[at, :] += dk
                dv_s[at, :] += dv
            ds_s[slot, at, :] = ds
            return dq

        repeat(0, (i + 1) * ratio, tile, 0, unrolled)

        def mix(j, dq):
            return dq + mm(columns(qkv_ref, 64, j, per), ds_s[slot, aligned(j, SPAN), :])

        dq = repeat(0, i + 1, mix, jnp.zeros((HEAD_DIM, SPAN), f32), unrolled)
        dq = (dq * score_scale).astype(bf16)
        for t in range(per):
            out_ref[i * per + t, 0:64, :] = dq[:, t * rows : (t + 1) * rows]
        return 0

    repeat(0, count, block, 0, unrolled)
    for j in range(blocks):
        at = slice(j * rows, (j + 1) * rows)
        dk = jnp.transpose(dk_s[at, :] * score_scale).astype(bf16)
        dv = jnp.transpose(dv_s[at, :]).astype(bf16)
        out_ref[j, 64:128, :] = dk
        out_ref[j, 128:192, :] = dv


def attend(qkv):
    blocks, _, rows = qkv.shape
    length = blocks * rows
    return pl.pallas_call(
        functools.partial(attend_kernel, length <= 2048),
        out_shape=(
            jax.ShapeDtypeStruct((blocks, HEAD_DIM, rows), bf16),
            jax.ShapeDtypeStruct((blocks, HEAD_DIM, rows), f32),
            jax.ShapeDtypeStruct((length // SPAN, 1, SPAN), f32),
        ),
        scratch_shapes=[
            pltpu.VMEM((length, HEAD_DIM), bf16),
            pltpu.VMEM((blocks, 1, rows), jnp.int32),
            pltpu.VMEM((2, length, SPAN), f32),
        ],
        compiler_params=pltpu.CompilerParams(vmem_limit_bytes=32 * 2**20),
        cost_estimate=pl.CostEstimate(
            flops=length * length * HEAD_DIM * 2,
            bytes_accessed=length * 1024,
            transcendentals=length * length // 2,
        ),
        name="attend",
    )(qkv)


def attend_back(qkv, grad, wide, lse):
    blocks, _, rows = qkv.shape
    length = blocks * rows
    return pl.pallas_call(
        functools.partial(attend_back_kernel, length <= 2048),
        out_shape=jax.ShapeDtypeStruct((blocks, 3 * HEAD_DIM, rows), bf16),
        scratch_shapes=[
            pltpu.VMEM((length, HEAD_DIM), bf16),
            pltpu.VMEM((length, HEAD_DIM), bf16),
            pltpu.VMEM((length, HEAD_DIM), bf16),
            pltpu.VMEM((length, HEAD_DIM), bf16),
            pltpu.VMEM((blocks, 1, rows), jnp.int32),
            pltpu.VMEM((blocks, 1, rows), f32),
            pltpu.VMEM((length, HEAD_DIM), f32),
            pltpu.VMEM((length, HEAD_DIM), f32),
            pltpu.VMEM((2, length, SPAN), bf16),
        ],
        compiler_params=pltpu.CompilerParams(vmem_limit_bytes=32 * 2**20),
        cost_estimate=pl.CostEstimate(
            flops=length * length * HEAD_DIM * 5,
            bytes_accessed=length * 2048,
            transcendentals=length * length // 2,
        ),
        name="attend_back",
    )(qkv, grad, wide, lse)


def feed_kernel(rows_ref, grad_ref, up_ref, down_ref, after_ref, out_ref, back_ref):
    step = pl.program_id(0)
    up, down = up_ref[...], down_ref[...]
    act, slope = gelu_pair(mm(rows_ref[...], up))
    out = mm(act.astype(bf16), down)
    inner = (mm(grad_ref[...], down, ((1,), (1,))) * slope).astype(bf16)
    back = mm(inner, up, ((1,), (1,)))

    @pl.when(step == 0)
    def _():
        out_ref[...] = out
        back_ref[...] = back

    @pl.when(step > 0)
    def _():
        out_ref[...] += out
        back_ref[...] += back


def feed(rows, grad, up, down, after, first, hidden):
    count, width = rows.shape
    chunk = min(hidden, 1024)
    skip = first // chunk
    whole = pl.BlockSpec((count, width), lambda c: (0, 0))
    return pl.pallas_call(
        feed_kernel,
        grid=(hidden // chunk,),
        in_specs=[
            whole,
            whole,
            pl.BlockSpec((width, chunk), lambda c: (0, c + skip)),
            pl.BlockSpec((chunk, width), lambda c: (c + skip, 0)),
            pl.BlockSpec(memory_space=pl.ANY),
        ],
        out_specs=[whole, whole],
        out_shape=[jax.ShapeDtypeStruct((count, width), f32)] * 2,
        compiler_params=pltpu.CompilerParams(vmem_limit_bytes=55 * 2**20),
        cost_estimate=pl.CostEstimate(
            flops=8 * count * width * hidden,
            bytes_accessed=4 * width * hidden,
            transcendentals=count * hidden,
        ),
        name="feed",
    )(rows, grad, up, down, after)


def begin_kernel(x_ref, label_ref, gain_ref, shift_ref, weight_ref, a_ref, out_ref):
    step = pl.program_id(0)
    groups = 2

    @pl.when(step == 0)
    def _():
        normed, _ = norm_stats(x_ref[...].astype(f32))
        a_ref[...] = (normed * gain_ref[...] + shift_ref[...]).astype(bf16)
        labels = label_ref[...].astype(f32).astype(bf16)
        for head in range(HEADS):
            out_ref[head, 192:208, :] = jnp.broadcast_to(labels, (16, labels.shape[1]))

    heads = HEADS // groups
    columns = jnp.transpose(mm(a_ref[...], weight_ref[...])).astype(bf16)
    at = pl.ds(pl.multiple_of(step // groups * HEAD_DIM, HEAD_DIM), HEAD_DIM)
    for head in range(heads):
        part = columns[head * HEAD_DIM : (head + 1) * HEAD_DIM]
        out_ref[step % groups * heads + head, at, :] = part


def begin(x, labels, gain, shift, weight):
    rows, width = x.shape
    return pl.pallas_call(
        begin_kernel,
        grid=(6,),
        in_specs=[
            pl.BlockSpec((rows, width), lambda c: (0, 0)),
            pl.BlockSpec((1, rows), lambda c: (0, 0)),
            pl.BlockSpec((1, width), lambda c: (0, 0)),
            pl.BlockSpec((1, width), lambda c: (0, 0)),
            pl.BlockSpec((width, width // 2), lambda c: (0, c)),
        ],
        out_specs=[
            pl.BlockSpec((rows, width), lambda c: (0, 0)),
            pl.BlockSpec((HEADS, 208, rows), lambda c: (0, 0, 0)),
        ],
        out_shape=[
            jax.ShapeDtypeStruct((rows, width), bf16),
            jax.ShapeDtypeStruct((HEADS, 208, rows), bf16),
        ],
        compiler_params=pltpu.CompilerParams(vmem_limit_bytes=60 * 2**20),
        cost_estimate=pl.CostEstimate(
            flops=6 * rows * width * width, bytes_accessed=6 * width * width, transcendentals=0
        ),
        name="begin",
    )(x, labels, gain, shift, weight)


def choices(logits, experts):
    lane = lax.broadcasted_iota(jnp.int32, logits.shape, 1)
    total = jnp.zeros_like(logits)
    for low, high in ((0, experts), (experts, experts + 2)):
        inside = (lane >= low) & (lane < high)
        masked = jnp.where(inside, logits, masked_score)
        e = jnp.where(inside, jnp.exp(masked - jnp.max(masked, axis=1, keepdims=True)), 0.0)
        total = total + e / jnp.sum(e, axis=1, keepdims=True)
    return total, lane


def pick(values, lane, index):
    return jnp.sum(jnp.where(lane == index, values, 0.0), axis=1, keepdims=True)


def bf16_parts(value):
    high = value.astype(bf16).astype(f32)
    rest = value - high
    middle = rest.astype(bf16).astype(f32)
    return [high, middle, rest - middle]


def middle_kernel(
    o_ref, weight_ref, x_ref, dy_ref, gain_ref, shift_ref, choose_ref, bias_ref, info_ref,
    dispatch_ref, hidden_ref, b_ref, rows_ref, slots_ref, dense_ref, scalar_ref,
):
    experts, slots, count = dispatch_ref.shape
    hidden = x_ref[...].astype(f32) + mm(o_ref[...], weight_ref[...], ((0,), (0,)))
    hidden_ref[...] = hidden
    normed, _ = norm_stats(hidden)
    b = (normed * gain_ref[...] + shift_ref[...]).astype(bf16)
    b_ref[...] = b
    rows_ref[0:count, :] = b
    dy = dy_ref[...]
    for e in range(experts):
        slots_ref[e, 0:slots, :] = mm(dispatch_ref[e], b).astype(bf16)
        slots_ref[e, slots : 2 * slots, :] = mm(dispatch_ref[e], dy).astype(bf16)
    values, lane = choices(mm(b, choose_ref[...]) + bias_ref[...], experts)
    info = info_ref[...]
    gate = pick(values, lane, info[:, 0:1].astype(jnp.int32))
    mixing = pick(values, lane, experts)
    other = pick(values, lane, experts + 1)
    scalar_ref[...] = jnp.where(lane == experts + 2, gate, values)
    dense_ref[...] = (mixing * dy.astype(f32)).astype(bf16)
    columns = bf16_parts(mixing) + bf16_parts(other * gate) + [info[:, 1:2], info[:, 1:2]]
    block = jnp.zeros_like(values)
    for k, column in enumerate(columns):
        block = jnp.where(lane == k, column, block)
    rows_ref[count:, :] = jnp.zeros((8, rows_ref.shape[1]), bf16)
    rows_ref[count:, 0:count] = jnp.transpose(block)[0:8].astype(bf16)


def middle(o, weight, x, dy, gain, shift, choose, bias, info, dispatch):
    rows, width = x.shape
    experts, slots, _ = dispatch.shape
    return pl.pallas_call(
        middle_kernel,
        out_shape=[
            jax.ShapeDtypeStruct((rows, width), f32),
            jax.ShapeDtypeStruct((rows, width), bf16),
            jax.ShapeDtypeStruct((rows + 8, width), bf16),
            jax.ShapeDtypeStruct((experts, 2 * slots, width), bf16),
            jax.ShapeDtypeStruct((rows, width), bf16),
            jax.ShapeDtypeStruct((rows, 128), f32),
        ],
        compiler_params=pltpu.CompilerParams(vmem_limit_bytes=32 * 2**20),
        cost_estimate=pl.CostEstimate(
            flops=4 * rows * width * width, bytes_accessed=4 * width * width, transcendentals=0
        ),
        name="middle",
    )(o, weight, x, dy, gain, shift, choose, bias, info, dispatch)


def expert_kernel(
    mine_ref, slots_ref, choose_ref, bias_ref, up_ref, down_ref, after_ref, out_ref,
    rows_s, grad_s, total_s, back_s,
):
    step = pl.program_id(0)
    sources, double, _ = slots_ref.shape
    slots = double // 2

    @pl.when(step == 0)
    def _():
        for n in range(sources):
            at = slice(n * slots, (n + 1) * slots)
            rows_s[at, :] = slots_ref[n, 0:slots, :]
            grad_s[at, :] = slots_ref[n, slots:double, :]
        values, lane = choices(mm(rows_s[...], choose_ref[...]) + bias_ref[...], sources)
        gate = pick(values, lane, mine_ref[0])
        other = pick(values, lane, sources + 1)
        grad_s[...] = (gate * (other * grad_s[...].astype(f32))).astype(bf16)
        total_s[...] = jnp.zeros_like(total_s)
        back_s[...] = jnp.zeros_like(back_s)

    up, down = up_ref[...], down_ref[...]
    act, slope = gelu_pair(mm(rows_s[...], up))
    total_s[...] += mm(act.astype(bf16), down)
    inner = (mm(grad_s[...], down, ((1,), (1,))) * slope).astype(bf16)
    back_s[...] += mm(inner, up, ((1,), (1,)))

    @pl.when(step == pl.num_programs(0) - 1)
    def _():
        for n in range(sources):
            at = slice(n * slots, (n + 1) * slots)
            out_ref[n, 0:slots, :] = total_s[at, :].astype(bf16)
            out_ref[n, slots:double, :] = back_s[at, :].astype(bf16)


def expert_feed(mine, slots, choose, bias, up, down, after):
    sources, double, width = slots.shape
    hidden = up.shape[1]
    chunk = min(hidden, 1024)
    count = sources * double // 2
    whole = pl.BlockSpec((sources, double, width), lambda c, m: (0, 0, 0))
    return pl.pallas_call(
        expert_kernel,
        grid_spec=pltpu.PrefetchScalarGridSpec(
            num_scalar_prefetch=1,
            grid=(hidden // chunk,),
            in_specs=[
                whole,
                pl.BlockSpec((width, 128), lambda c, m: (0, 0)),
                pl.BlockSpec((1, 128), lambda c, m: (0, 0)),
                pl.BlockSpec((width, chunk), lambda c, m: (0, c)),
                pl.BlockSpec((chunk, width), lambda c, m: (c, 0)),
                pl.BlockSpec(memory_space=pl.ANY),
            ],
            out_specs=whole,
            scratch_shapes=[
                pltpu.VMEM((count, width), bf16),
                pltpu.VMEM((count, width), bf16),
                pltpu.VMEM((count, width), f32),
                pltpu.VMEM((count, width), f32),
            ],
        ),
        out_shape=jax.ShapeDtypeStruct((sources, double, width), bf16),
        compiler_params=pltpu.CompilerParams(vmem_limit_bytes=55 * 2**20),
        cost_estimate=pl.CostEstimate(
            flops=8 * count * width * hidden,
            bytes_accessed=4 * width * hidden,
            transcendentals=count * hidden,
        ),
        name="expert_feed",
    )(mine, slots, choose, bias, up, down, after)


def combine_kernel(
    back_ref, dispatch_ref, hidden_ref, rows_ref, dy_ref, first_ref, first_back_ref, second_ref,
    second_back_ref, scalar_ref, info_ref, gain_ref, choose_ref, weight_ref,
    result_ref, grad_ref, low_ref, heads_ref, sums_ref, bias_ref,
):
    experts, slots, count = dispatch_ref.shape
    raw, grad_b = None, first_back_ref[...] + second_back_ref[...]
    for e in range(experts):
        part = mm(dispatch_ref[e], back_ref[e, 0:slots, :], ((0,), (0,)))
        raw = part if raw is None else raw + part
        grad_b = grad_b + mm(dispatch_ref[e], back_ref[e, slots : 2 * slots, :], ((0,), (0,)))
    hidden = hidden_ref[...]
    dy = dy_ref[...].astype(f32)
    scalars = scalar_ref[...]
    lane = lax.broadcasted_iota(jnp.int32, scalars.shape, 1)
    gate = pick(scalars, lane, experts + 2)
    mixing, other = pick(scalars, lane, experts), pick(scalars, lane, experts + 1)
    dense = first_ref[...] + second_ref[...]
    expert = gate * raw
    result_ref[...] = (hidden + mixing * dense + other * expert).astype(bf16)
    grad_gate = jnp.sum(other * dy * raw, axis=1, keepdims=True)
    grad_mixing = jnp.sum(dy * dense, axis=1, keepdims=True)
    grad_other = jnp.sum(dy * expert, axis=1, keepdims=True)
    mean = mixing * grad_mixing + other * grad_other
    onehot = (lane == info_ref[...][:, 0:1].astype(jnp.int32)).astype(f32)
    logits = jnp.where(lane < experts, scalars * (onehot - gate) * grad_gate, 0.0)
    logits = jnp.where(lane == experts, mixing * (grad_mixing - mean), logits)
    logits = jnp.where(lane == experts + 1, other * (grad_other - mean), logits)
    bias_ref[...] = jnp.sum(logits, axis=0, keepdims=True)
    b = rows_ref[...].astype(f32)
    sums_ref[...] = jnp.zeros_like(sums_ref)
    for e in range(experts + 2):
        column = logits[:, e : e + 1]
        grad_b = grad_b + column * choose_ref[e : e + 1, :].astype(f32)
        sums_ref[2 + e : 3 + e, :] = jnp.sum(column * b, axis=0, keepdims=True)
    normed, rstd = norm_stats(hidden)
    sums_ref[0:1, :] = jnp.sum(grad_b * normed, axis=0, keepdims=True)
    sums_ref[1:2, :] = jnp.sum(grad_b, axis=0, keepdims=True)
    grad = dy + norm_back(grad_b, gain_ref[...], normed, rstd)
    grad_ref[...] = grad
    low = grad.astype(bf16)
    low_ref[...] = low
    heads_ref[...] = mm(weight_ref[...], low, ((1,), (1,))).astype(bf16)


def combine(*operands):
    dispatch, hidden = operands[1], operands[2]
    rows, width = hidden.shape
    lines = 8 * (1 + (dispatch.shape[0] + 3) // 8)
    return pl.pallas_call(
        combine_kernel,
        out_shape=[
            jax.ShapeDtypeStruct((rows, width), bf16),
            jax.ShapeDtypeStruct((rows, width), f32),
            jax.ShapeDtypeStruct((rows, width), bf16),
            jax.ShapeDtypeStruct((width, rows), bf16),
            jax.ShapeDtypeStruct((lines, width), f32),
            jax.ShapeDtypeStruct((1, 128), f32),
        ],
        compiler_params=pltpu.CompilerParams(vmem_limit_bytes=32 * 2**20),
        cost_estimate=pl.CostEstimate(
            flops=4 * rows * width * width, bytes_accessed=4 * width * width, transcendentals=0
        ),
        name="combine",
    )(*operands)


def slice_kernel(
    dense_units, mine_ref, rows_ref, grad_ref, up_ref, down_ref, up_out, down_out, up_acc, down_acc
):
    step = pl.program_id(0)
    per, count = grad_ref.shape[:2]

    @pl.when(step == 0)
    def _():
        up_acc[...] = jnp.zeros_like(up_acc)
        down_acc[...] = jnp.zeros_like(down_acc)

    rows, dense_grad, expert_grad = [], [], []
    for t in range(per):
        scalars = jnp.transpose(rows_ref[t, count : count + 8, 0:count].astype(f32))
        mixing = scalars[:, 0:1] + scalars[:, 1:2] + scalars[:, 2:3]
        gate = scalars[:, 3:4] + scalars[:, 4:5] + scalars[:, 5:6]
        mine = scalars[:, 6:7] == mine_ref[0].astype(f32)
        grad = grad_ref[t].astype(f32)
        rows.append(rows_ref[t, 0:count, :])
        dense_grad.append((mixing * grad).astype(bf16))
        expert_grad.append((jnp.where(mine, gate, 0.0) * grad).astype(bf16))
    rows = jnp.concatenate(rows, axis=0)
    dense_grad = jnp.concatenate(dense_grad, axis=0)
    expert_grad = jnp.concatenate(expert_grad, axis=0)
    act, slope = gelu_pair(mm(rows, up_ref[...]))
    act = act.astype(bf16)
    inner = jnp.concatenate(
        [mm(dense_grad, down_ref[:, :dense_units]), mm(expert_grad, down_ref[:, dense_units:])],
        axis=1,
    )
    inner = (inner * slope).astype(bf16)
    first = ((0,), (0,))
    up_acc[...] += mm(inner, rows, first)
    down_acc[:dense_units, :] += mm(act[:, :dense_units], dense_grad, first)
    down_acc[dense_units:, :] += mm(act[:, dense_units:], expert_grad, first)

    @pl.when(step == pl.num_programs(0) - 1)
    def _():
        up = jnp.transpose(up_acc[...]).astype(bf16)
        own = up_out.shape[2]
        for chunk in range(up_out.shape[1]):
            lanes = up[:, chunk * 128 : (chunk + 1) * 128]
            up_out[:, chunk] = lanes.reshape(up_out.shape[0], own, 128)
        down_out[...] = down_acc[...]


def slice_grads(mine, rows, grad, up, down, dense_units, wide):
    devices, padded, width = rows.shape
    count = grad.shape[1]
    units = up.shape[1]
    per = 4
    fixed = pl.BlockSpec((width, units), lambda c, m: (0, 0))
    return pl.pallas_call(
        functools.partial(slice_kernel, dense_units),
        grid_spec=pltpu.PrefetchScalarGridSpec(
            num_scalar_prefetch=1,
            grid=(devices // per,),
            in_specs=[
                pl.BlockSpec((per, padded, width), lambda c, m: (c, 0, 0)),
                pl.BlockSpec((per, count, width), lambda c, m: (c, 0, 0)),
                fixed,
                fixed,
            ],
            out_specs=[
                pl.BlockSpec((wide, units // 128, width // wide, 128), lambda c, m: (0, 0, 0, 0)),
                pl.BlockSpec((units, width), lambda c, m: (0, 0)),
            ],
            scratch_shapes=[pltpu.VMEM((units, width), f32), pltpu.VMEM((units, width), f32)],
        ),
        out_shape=[
            jax.ShapeDtypeStruct((wide, units // 128, width // wide, 128), bf16),
            jax.ShapeDtypeStruct((units, width), f32),
        ],
        compiler_params=pltpu.CompilerParams(vmem_limit_bytes=55 * 2**20),
        cost_estimate=pl.CostEstimate(
            flops=8 * devices * count * width * units,
            bytes_accessed=4 * devices * count * width,
            transcendentals=devices * count * units,
        ),
        name="slice_grads",
    )(mine, rows, grad, up, down)


def product_sum(left_ref, array_ref):
    blocks, rows, width = array_ref.shape
    total = None
    for p in range(0, blocks, 2):
        left = jnp.concatenate([left_ref[p], left_ref[p + 1]], axis=1)
        part = mm(left, array_ref[p : p + 2].reshape(2 * rows, width))
        total = part if total is None else total + part
    return total


def in_kernel(left_ref, array_ref, out_ref):
    total = jnp.transpose(product_sum(left_ref, array_ref)).astype(bf16)
    wide, _, lanes = out_ref.shape
    own = total.shape[0] // wide
    for w in range(wide):
        rows = total[w * own : (w + 1) * own]
        out_ref[w, 0:own, :] = rows[:, 0:128]
        out_ref[w, own : own + own // 2, :] = jnp.concatenate(
            [rows[: own // 2, 128:192], rows[own // 2 :, 128:192]], axis=1
        )


def block_products(kernel, name, out_shape, left, array):
    blocks, rows, width = array.shape
    return pl.pallas_call(
        kernel,
        in_specs=[pl.BlockSpec(memory_space=pltpu.VMEM)] * 2,
        out_shape=jax.ShapeDtypeStruct(out_shape, bf16),
        compiler_params=pltpu.CompilerParams(vmem_limit_bytes=32 * 2**20),
        cost_estimate=pl.CostEstimate(
            flops=2 * blocks * rows * width * left.shape[1],
            bytes_accessed=2 * blocks * rows * width,
            transcendentals=0,
        ),
        name=name,
    )(left, array)


def finish_kernel(
    first_ref, got_ref, got_other_ref, ups_ref, ups_other_ref, in_out, dense_out, expert_out, sum_out
):
    wide = got_ref.shape[0]
    own = in_out.shape[0]
    first = first_ref[0] == 0
    half = own // 2
    sums = None
    for w in range(wide):
        total = got_ref[w].astype(f32) + got_other_ref[w].astype(f32)
        head = w * HEAD_DIM
        in_out[:, head : head + 64] = total[:own, :64]
        in_out[:, 1024 + head : 1024 + head + 64] = total[:own, 64:]
        in_out[:half, 2048 + head : 2048 + head + 64] = total[own : own + half, :64]
        in_out[half:, 2048 + head : 2048 + head + 64] = total[own : own + half, 64:]
        small = total[own + half :]
        sums = small if sums is None else sums + small
        mine, theirs = ups_ref[w, :own].astype(f32), ups_other_ref[w].astype(f32)
        dense_out[:, w * 256 : w * 256 + 128] = jnp.where(first, mine, theirs)
        dense_out[:, w * 256 + 128 : w * 256 + 256] = jnp.where(first, theirs, mine)
        expert_out[:, w * 256 : w * 256 + 128] = ups_ref[w, own : 2 * own].astype(f32)
        expert_out[:, w * 256 + 128 : w * 256 + 256] = ups_ref[w, 2 * own :].astype(f32)
    sum_out[...] = sums


def finish(first, got, got_other, ups, ups_other, own, hidden):
    width = HEADS * HEAD_DIM
    return pl.pallas_call(
        finish_kernel,
        in_specs=[pl.BlockSpec(memory_space=pltpu.SMEM)]
        + [pl.BlockSpec(memory_space=pltpu.VMEM)] * 4,
        out_shape=[
            jax.ShapeDtypeStruct((own, 3 * width), f32),
            jax.ShapeDtypeStruct((own, hidden), f32),
            jax.ShapeDtypeStruct((own, hidden), f32),
            jax.ShapeDtypeStruct((8, 128), f32),
        ],
        compiler_params=pltpu.CompilerParams(vmem_limit_bytes=32 * 2**20),
        name="finish",
    )(first, got, got_other, ups, ups_other)


def after(value, *others):
    return lax.optimization_barrier((value,) + others)[0]


def gather(value):
    return lax.all_gather(value, WIDE, axis=0, tiled=True)


def exchange(columns):
    wide = lax.axis_size("chip") * lax.axis_size("core")
    blocks = columns.astype(bf16).reshape(wide, columns.shape[0] // wide, columns.shape[1])
    got = lax.all_to_all(blocks, WIDE, 0, 0, tiled=True)
    return got.transpose(1, 0, 2).reshape(blocks.shape[1], wide * blocks.shape[2])


def plain_slice(rows, grad, up, down):
    act, slope = gelu_pair(mm(rows, up))
    inner = (mm(grad, down, ((1,), (1,))) * slope).astype(bf16)
    return mm(rows, inner, ((0,), (0,))), mm(act.astype(bf16), grad, ((0,), (0,)))


def other_narrow(value):
    size = lax.axis_size("narrow")
    if size != 2:
        return lax.all_gather(value, "narrow", axis=0, tiled=False)
    swapped = lax.ppermute(value, "narrow", [(0, 1), (1, 0)])
    first = lax.axis_index("narrow") == 0
    return jnp.stack([jnp.where(first, value, swapped), jnp.where(first, swapped, value)])


def local(
    tokens, document, routing, capacity, load_before, first_gain, first_shift, project_in,
    project_out, second_gain, second_shift, dense_up, dense_down, router, mixer, mixer_bias,
    expert_up, expert_down, cotangent,
):
    rows, seq_count, width = tokens.shape
    assert seq_count == 1 and width == HEADS * HEAD_DIM
    chips, cores, narrow = (lax.axis_size(axis) for axis in ALL)
    wide = chips * cores
    devices = wide * narrow
    experts = capacity.shape[0]
    hidden_units = dense_up.shape[1]
    assert experts == narrow and wide % HEADS == 0 and cores == 2
    copies = wide // HEADS
    own = width // wide
    core = lax.axis_index("core")
    my_wide = lax.axis_index("chip") * cores + core
    my_narrow = lax.axis_index("narrow")
    swap = [(0, 1), (1, 0)]
    gather_all = wide == HEADS and narrow == 2

    grad_low = cotangent.reshape(rows, width)
    if gather_all:
        grad_all = lax.all_gather(grad_low, ALL, axis=0, tiled=False)

    chosen = routing.reshape(rows)
    onehot = (chosen[:, None] == jnp.arange(experts, dtype=jnp.int32)[None, :]).astype(jnp.int32)
    earlier = jnp.cumsum(onehot, axis=0) - onehot
    slot_rank = jnp.sum(earlier * onehot, axis=-1)
    kept = slot_rank < jnp.sum(capacity[None, :] * onehot, axis=-1)
    counts = jnp.sum(onehot * kept[:, None].astype(jnp.int32), axis=0)
    slots = -(-(rows * 5 // (4 * experts)) // 16) * 16
    slot_index = chosen * slots + slot_rank
    dispatch = (
        (slot_index[None, :] == jnp.arange(experts * slots, dtype=jnp.int32)[:, None])
        & kept[None, :]
    ).astype(bf16)
    dispatch = dispatch.reshape(experts, slots, rows)
    code = jnp.where(kept, chosen, experts)
    info = jnp.stack([chosen, code] + [code] * 6, axis=1).astype(f32)
    choose = jnp.concatenate([router, mixer], axis=1)
    choose = jnp.pad(choose, ((0, 0), (0, 128 - experts - 2)))
    bias = jnp.pad(mixer_bias, (experts, 126 - experts)).reshape(1, 128)

    x = tokens.reshape(rows, width)
    a, payload = begin(
        x,
        document.reshape(1, rows),
        first_gain.reshape(1, width),
        first_shift.reshape(1, width),
        project_in,
    )
    payload = jnp.repeat(payload, copies, axis=0)
    qkv = lax.all_to_all(payload, WIDE, 0, 0, tiled=True)
    expert_units, dense_units = hidden_units // wide, hidden_units // devices
    my_up = expert_up.reshape(width, hidden_units)
    my_down = expert_down.reshape(hidden_units, width)
    up_slice = lax.dynamic_slice_in_dim(my_up, my_wide * expert_units, expert_units, axis=1)
    down_slice = lax.dynamic_slice_in_dim(my_down, my_wide * expert_units, expert_units, axis=0)
    if gather_all:
        dense_first = my_wide * expert_units + my_narrow * dense_units
        dense_up_slice = lax.dynamic_slice_in_dim(dense_up, dense_first, dense_units, axis=1)
        dense_down_slice = lax.dynamic_slice_in_dim(dense_down, dense_first, dense_units, axis=0)
        ups = jnp.concatenate([dense_up_slice, up_slice], axis=1)
        downs = jnp.concatenate([dense_down_slice, down_slice], axis=0).T
        qkv = after(qkv, ups, downs)
    qkv = after(qkv, dispatch, info, choose, bias)
    head_low, head_wide, lse = attend(qkv)
    attended = lax.all_to_all(head_low, WIDE, 0, 0, tiled=True)[::copies].reshape(width, rows)

    hidden, b, rows_sent, slots_sent, dense_grad, scalars = middle(
        attended,
        project_out,
        x,
        grad_low,
        second_gain.reshape(1, width),
        second_shift.reshape(1, width),
        choose,
        bias,
        info,
        dispatch,
    )
    slots_got = lax.all_to_all(slots_sent, "narrow", 0, 0, tiled=True)
    half_units = hidden_units // 2
    dense_res, dense_back = feed(b, dense_grad, dense_up, dense_down, capacity, 0, half_units)
    if gather_all:
        rows_all = lax.all_gather(
            after(rows_sent, grad_all, slots_got, dense_res), ALL, axis=0, tiled=False
        )
    my_place = my_narrow.astype(jnp.int32).reshape(1)
    slots_back = expert_feed(my_place, slots_got, choose, bias, my_up, my_down, dense_res)
    returned = lax.all_to_all(slots_back, "narrow", 0, 0, tiled=True)
    dense_more, back_more = feed(
        b, dense_grad, dense_up, dense_down, slots_back, half_units, half_units
    )
    result, grad_hidden, grad_attn, grad_heads, second_sums, bias_part = combine(
        returned,
        dispatch,
        hidden,
        b,
        grad_low,
        dense_res,
        dense_back,
        dense_more,
        back_more,
        scalars,
        info,
        second_gain.reshape(1, width),
        choose.T,
        project_out,
    )
    result = result.reshape(rows, 1, width)

    grad_heads = grad_heads.reshape(HEADS, HEAD_DIM, rows)
    grad_heads = jnp.repeat(grad_heads, copies, axis=0)
    head_grad = lax.all_to_all(grad_heads, WIDE, 0, 0, tiled=True)
    small_part = second_sums[2 : 4 + experts].T
    bias_part = bias_part[0, experts : experts + 2]
    grad_blocks = attend_back(qkv, head_grad, head_wide, lse)
    if gather_all:
        a = after(a, rows_all, grad_blocks)
    a_all = lax.all_gather(a, WIDE, axis=0, tiled=False)
    sent_back = lax.all_to_all(grad_blocks, WIDE, 0, 0, tiled=True)[::copies]

    if gather_all:
        ups_part, downs_part = slice_grads(
            my_narrow.astype(jnp.int32).reshape(1), rows_all, grad_all, ups, downs, dense_units, wide
        )
        expert_down_grad = downs_part[dense_units:].reshape(expert_units, 1, width)
        dense_down_grad = other_narrow(downs_part[:dense_units].astype(bf16)).astype(f32)
        dense_down_grad = dense_down_grad.reshape(narrow * dense_units, width)

        ups_got = lax.all_to_all(ups_part.reshape(wide, -1, 128), WIDE, 0, 0, tiled=True)
        ups_other = lax.ppermute(ups_got[:, :own], "narrow", swap)
        sent_back = after(sent_back, ups_part)
        out_part = mm(after(attended, ups_part), grad_attn).reshape(chips, cores, own, width)
        mine = lax.dynamic_index_in_dim(out_part, core, axis=1, keepdims=False)
        theirs = lax.dynamic_index_in_dim(out_part, 1 - core, axis=1, keepdims=False)
        out_part = mine + lax.ppermute(theirs.astype(bf16), "core", swap).astype(f32)
        out_part = out_part.reshape(chips, narrow, own // narrow, width)
        mine = lax.dynamic_index_in_dim(out_part, my_narrow, axis=1, keepdims=False)
        theirs = lax.dynamic_index_in_dim(out_part, 1 - my_narrow, axis=1, keepdims=False)
        out_part = mine + lax.ppermute(theirs.astype(bf16), "narrow", swap).astype(f32)
        out_part = out_part.astype(bf16)

    grad_qkv = sent_back.reshape(HEADS, 3, HEAD_DIM, rows).transpose(1, 0, 2, 3)
    grad_qkv = grad_qkv.reshape(3 * width, rows)
    grad_a = mm(grad_qkv, project_in, ((0,), (1,)))
    normed_one, rstd_one = norm_stats(x.astype(f32))
    first_gain_part = jnp.sum(grad_a * normed_one, axis=0)
    first_shift_part = jnp.sum(grad_a, axis=0)
    input_grad = grad_hidden + norm_back(grad_a, first_gain, normed_one, rstd_one)
    input_grad = input_grad.astype(bf16).reshape(rows, 1, width)

    vectors = jnp.stack([first_gain_part, first_shift_part, second_sums[0], second_sums[1]])
    if gather_all:
        out_part = lax.all_to_all(after(out_part, ups_got), "chip", 0, 0, tiled=True)
        out_part = jnp.sum(out_part.astype(f32), axis=0).astype(bf16)
        project_out_grad = other_narrow(out_part).astype(f32).reshape(own, width)

        in_part = block_products(
            in_kernel, "in_grad", (wide, own * 3 // 2, 128), grad_blocks, a_all
        )
        vectors = vectors.reshape(4, wide, own).transpose(1, 0, 2).reshape(wide, 4 * own)
        small = small_part.reshape(wide, own, experts + 2).transpose(0, 2, 1)
        small = small.reshape(wide, own * (experts + 2))
        bias_parts = jnp.stack(three_parts(bias_part)).reshape(1, 6)
        bias_parts = jnp.broadcast_to(jnp.pad(bias_parts, ((0, 0), (0, 506))), (wide, 512))
        flat = jnp.concatenate([vectors, small, bias_parts], axis=1).astype(bf16)
        sent = jnp.concatenate([in_part, flat.reshape(wide, 8, 128)], axis=1)
        got = lax.all_to_all(after(sent, ups_got), WIDE, 0, 0, tiled=True)
        got_other = lax.ppermute(got, "narrow", swap)
        project_in_grad, dense_up_grad, expert_up_grad, sums = finish(
            my_narrow.astype(jnp.int32).reshape(1), got, got_other, ups_got, ups_other, own, hidden_units
        )
        expert_up_grad = expert_up_grad.reshape(own, 1, hidden_units)
        sums = sums.reshape(-1)
        vector_sums = sums[: 4 * own].reshape(4, own)
        small_sum = sums[4 * own : own * (6 + experts)].reshape(experts + 2, own).T
        bias_at = own * (6 + experts)
        mixer_bias_grad = jnp.sum(sums[bias_at : bias_at + 6].reshape(3, 2), axis=0)

        codes = rows_all[:, rows + 6, :rows].astype(f32).reshape(devices * rows, 1)
        count_sum = jnp.sum((codes == jnp.arange(experts, dtype=f32)[None, :]).astype(f32), axis=0)
    else:
        def wide_sum(part):
            part = lax.psum_scatter(part.astype(bf16), WIDE, scatter_dimension=0, tiled=True)
            return lax.psum(part, "narrow").astype(f32)

        project_out_grad = wide_sum(mm(attended, grad_attn))
        dense_up_slice = lax.dynamic_slice_in_dim(
            dense_up, my_wide * expert_units, expert_units, axis=1
        )
        dense_down_slice = lax.dynamic_slice_in_dim(
            dense_down, my_wide * expert_units, expert_units, axis=0
        )
        slot_rows = slots_got[:, :slots].reshape(narrow * slots, width)
        slot_values, lane = choices(mm(slot_rows, choose) + bias, experts)
        slot_scale = pick(slot_values, lane, my_narrow), pick(slot_values, lane, experts + 1)
        slot_grads = slots_got[:, slots:].reshape(narrow * slots, width).astype(f32)
        slot_grads = (slot_scale[0] * (slot_scale[1] * slot_grads)).astype(bf16)
        dense_up_part, dense_down_part = plain_slice(
            gather(b), gather(dense_grad), dense_up_slice, dense_down_slice
        )
        dense_down_grad = lax.psum(dense_down_part.astype(bf16), "narrow").astype(f32)
        dense_up_grad = lax.psum(exchange(dense_up_part), "narrow").astype(f32)
        expert_up_part, expert_down_grad = plain_slice(
            gather(slot_rows), gather(slot_grads), up_slice, down_slice
        )
        expert_down_grad = expert_down_grad.reshape(expert_units, 1, width)
        expert_up_grad = exchange(expert_up_part).astype(f32).reshape(own, 1, hidden_units)

        flat = grad_blocks.transpose(1, 0, 2).reshape(3 * HEAD_DIM, wide * rows)
        in_part = mm(flat, a_all.reshape(wide * rows, width)).astype(bf16)
        in_part = in_part.reshape(3 * HEAD_DIM, wide, own).transpose(1, 0, 2)
        in_part = lax.all_to_all(in_part, WIDE, 0, 0, tiled=True)[::copies]
        in_part = in_part.reshape(HEADS, 3, HEAD_DIM, own).transpose(3, 1, 0, 2)
        project_in_grad = lax.psum(in_part.reshape(own, 3 * width), "narrow").astype(f32)
        vector_sums = wide_sum(vectors.T).T
        small_sum = wide_sum(small_part)
        mixer_bias_grad = lax.psum(bias_part, ALL)
        count_sum = lax.psum(counts.astype(f32), ALL)

    load_after = momentum * load_before + (1.0 - momentum) * (
        count_sum * experts / (devices * rows)
    )
    return (
        result, input_grad, vector_sums[0], vector_sums[1], project_in_grad, project_out_grad,
        vector_sums[2], vector_sums[3], dense_up_grad, dense_down_grad, small_sum[:, :experts],
        small_sum[:, experts:], mixer_bias_grad, expert_up_grad, expert_down_grad, load_after,
    )


def solution(mesh):
    wide, narrow = mesh.devices.shape
    fine = Mesh(mesh.devices.reshape(wide // 2, 2, narrow), ALL)
    by_token = P(WIDE, "narrow", None)
    by_expert = P(None, "narrow", None)
    return jax.shard_map(
        local,
        mesh=fine,
        in_specs=(
            by_token, P(WIDE, "narrow"), by_token, P(), P(), P(), P(), P(), P(), P(), P(), P(),
            P(), P(), P(), P(), by_expert, by_expert, by_token,
        ),
        out_specs=(
            by_token, by_token, P(WIDE), P(WIDE), P(WIDE, None), P(WIDE, None), P(WIDE), P(WIDE),
            P(WIDE, None), P(WIDE, None), P(WIDE, None), P(WIDE, None), P(), by_token, by_token,
            P(),
        ),
        check_vma=False,
    )
```

```python
import functools

import jax
import jax.numpy as jnp
from jax import lax
from jax.experimental import pallas as pl
from jax.experimental.pallas import tpu as pltpu
from jax.sharding import Mesh, PartitionSpec as P

HEADS = 16
HEAD_DIM = 64
WIDE = ("chip", "core")
ALL = ("chip", "core", "narrow")

SHRINK = 1
score_scale = 0.125
norm_eps = 1e-05
momentum = 0.3
masked_score = -1e30
gelu_slope = 0.7978845608028654
gelu_cubic = 0.044715

f32 = jnp.float32
bf16 = jnp.bfloat16


def mm(left, right, dims=((1,), (0,))):
    return lax.dot_general(left, right, (dims, ((), ())), preferred_element_type=f32)


def estimate(flops, bytes_accessed, transcendentals):
    return pl.CostEstimate(
        flops=flops // SHRINK,
        bytes_accessed=bytes_accessed // SHRINK,
        transcendentals=transcendentals // SHRINK,
    )


def norm_stats(rows):
    average = jnp.mean(rows, axis=-1, keepdims=True)
    centered = rows - average
    variance = jnp.mean(centered * centered, axis=-1, keepdims=True)
    rstd = lax.rsqrt(variance + norm_eps)
    return centered * rstd, rstd


def norm_back(grad, gain, normed, rstd):
    scaled = grad * gain
    mean_scaled = jnp.mean(scaled, axis=-1, keepdims=True)
    mean_product = jnp.mean(scaled * normed, axis=-1, keepdims=True)
    return rstd * (scaled - mean_scaled - normed * mean_product)


def gelu_pair(u):
    square = u * u
    t = jnp.tanh(gelu_slope * u * (1.0 + gelu_cubic * square))
    half = 0.5 * (1.0 + t)
    slope = half + 0.5 * u * (1.0 - t * t) * (gelu_slope * (1.0 + 3.0 * gelu_cubic * square))
    return u * half, slope


def three_parts(value):
    high = lax.reduce_precision(value, 8, 7)
    rest = value - high
    middle = lax.reduce_precision(rest, 8, 7)
    low = lax.reduce_precision(rest - middle, 8, 7)
    return high, middle, low


SPAN = 256
TILE = 256


def columns(ref, first, block, per):
    return jnp.concatenate(
        [ref[block * per + t, first : first + HEAD_DIM, :] for t in range(per)], axis=1
    )


def rows_of(values):
    return jnp.transpose(values.astype(f32)).astype(bf16)


def fold(tile, op):
    return op(tile.reshape(tile.shape[0] // 8, 8, tile.shape[1]), axis=0)


def repeat(low, high, body, carry, unrolled):
    if unrolled:
        for step in range(low, high):
            carry = body(step, carry)
        return carry
    return lax.fori_loop(low, high, body, carry)


def aligned(index, size):
    start = index * size
    return pl.ds(start if isinstance(index, int) else pl.multiple_of(start, size), size)


def document_starts(qkv_ref, start_s):
    labels = [qkv_ref[j, 192:208, :].astype(f32)[0:1] for j in range(qkv_ref.shape[0])]
    every = jnp.concatenate(labels, axis=0)
    counts = [jnp.sum((every < v).astype(f32), keepdims=True) for v in range(1, 5)]
    before = [jnp.zeros_like(counts[0])] + counts[:-1]
    start = sum(
        jnp.where(every >= v + 1, counts[v] - before[v], 0.0) for v in range(4)
    ).astype(jnp.int32)
    for j in range(qkv_ref.shape[0]):
        start_s[j] = start[j : j + 1]


def allowed(first_key, start, first_query, row_at, column_at, diagonal):
    keep = row_at >= start - first_key
    if diagonal is None or diagonal:
        keep = keep & (row_at - column_at <= first_query - first_key)
    return keep


def attend_kernel(unrolled, qkv_ref, low_ref, wide_ref, lse_ref, key_s, start_s, score_s):
    blocks, _, rows = qkv_ref.shape
    per = SPAN // rows
    count, ratio = blocks // per, SPAN // TILE
    for j in range(blocks):
        key_s[j * rows : (j + 1) * rows, :] = rows_of(qkv_ref[j, 64:128, :])
    document_starts(qkv_ref, start_s)
    shape = (TILE, SPAN)
    row_at = lax.broadcasted_iota(jnp.int32, shape, 0)
    column_at = lax.broadcasted_iota(jnp.int32, shape, 1)

    def block(i, _):
        query = (columns(qkv_ref, 0, i, per).astype(f32) * score_scale).astype(bf16)
        start = jnp.concatenate([start_s[i * per + t] for t in range(per)], axis=1)
        slot = i % 2

        def score(j, peak):
            at = aligned(j, TILE)
            s = mm(key_s[at, :], query)
            diagonal = j >= i * ratio if unrolled else None
            keep = allowed(j * TILE, start, i * SPAN, row_at, column_at, diagonal)
            s = jnp.where(keep, s, masked_score)
            score_s[slot, at, :] = s
            return jnp.maximum(peak, fold(s, jnp.max))

        end = (i + 1) * ratio
        peak = repeat(0, end, score, jnp.full((8, SPAN), masked_score, f32), unrolled)
        peak = jnp.max(peak, axis=0, keepdims=True)

        def weigh(j, total):
            at = aligned(j, TILE)
            e = jnp.exp(score_s[slot, at, :] - peak)
            score_s[slot, at, :] = e
            return total + fold(e, jnp.sum)

        total = repeat(0, end, weigh, jnp.zeros((8, SPAN), f32), unrolled)
        total = jnp.sum(total, axis=0, keepdims=True)
        share = 1.0 / total

        def mix(j, out):
            p = (score_s[slot, aligned(j, SPAN), :] * share).astype(bf16)
            return out + mm(columns(qkv_ref, 128, j, per), p)

        out = repeat(0, i + 1, mix, jnp.zeros((HEAD_DIM, SPAN), f32), unrolled)
        for t in range(per):
            part = out[:, t * rows : (t + 1) * rows]
            wide_ref[i * per + t] = part
            low_ref[i * per + t] = part.astype(bf16)
        lse_ref[i] = peak + jnp.log(total)
        return 0

    repeat(0, count, block, 0, unrolled)


def attend_back_kernel(
    unrolled, qkv_ref, do_ref, wide_ref, lse_ref, out_ref,
    query_s, key_s, value_s, grad_s, start_s, delta_s, dk_s, dv_s, ds_s,
):
    blocks, _, rows = qkv_ref.shape
    per = SPAN // rows
    count, ratio = blocks // per, SPAN // TILE
    for j in range(blocks):
        at = slice(j * rows, (j + 1) * rows)
        query_s[at, :] = rows_of(qkv_ref[j, 0:64, :])
        key_s[at, :] = rows_of(qkv_ref[j, 64:128, :])
        value_s[at, :] = rows_of(qkv_ref[j, 128:192, :])
        grad_s[at, :] = rows_of(do_ref[j])
        delta_s[j] = jnp.sum(do_ref[j].astype(f32) * wide_ref[j], axis=0, keepdims=True)
    document_starts(qkv_ref, start_s)
    shape = (TILE, SPAN)
    row_at = lax.broadcasted_iota(jnp.int32, shape, 0)
    column_at = lax.broadcasted_iota(jnp.int32, shape, 1)
    if not unrolled:
        dk_s[...] = jnp.zeros_like(dk_s)
        dv_s[...] = jnp.zeros_like(dv_s)

    def block(i, _):
        query = (columns(qkv_ref, 0, i, per).astype(f32) * score_scale).astype(bf16)
        grad = jnp.concatenate([do_ref[i * per + t] for t in range(per)], axis=1)
        start = jnp.concatenate([start_s[i * per + t] for t in range(per)], axis=1)
        delta = jnp.concatenate([delta_s[i * per + t] for t in range(per)], axis=1)
        lse = lse_ref[i]
        query_rows, grad_rows = query_s[aligned(i, SPAN), :], grad_s[aligned(i, SPAN), :]
        slot = i % 2

        def tile(j, dq):
            at = aligned(j, TILE)
            s = mm(key_s[at, :], query)
            diagonal = j >= i * ratio if unrolled else None
            keep = allowed(j * TILE, start, i * SPAN, row_at, column_at, diagonal)
            p = jnp.where(keep, jnp.exp(s - lse), 0.0)
            ds = (p * (mm(value_s[at, :], grad) - delta)).astype(bf16)
            p = p.astype(bf16)
            dk, dv = mm(ds, query_rows), mm(p, grad_rows)
            if unrolled and diagonal:
                dk_s[at, :] = dk
                dv_s[at, :] = dv
            else:
                dk_s[at, :] += dk
                dv_s[at, :] += dv
            ds_s[slot, at, :] = ds
            return dq

        repeat(0, (i + 1) * ratio, tile, 0, unrolled)

        def mix(j, dq):
            return dq + mm(columns(qkv_ref, 64, j, per), ds_s[slot, aligned(j, SPAN), :])

        dq = repeat(0, i + 1, mix, jnp.zeros((HEAD_DIM, SPAN), f32), unrolled)
        dq = (dq * score_scale).astype(bf16)
        for t in range(per):
            out_ref[i * per + t, 0:64, :] = dq[:, t * rows : (t + 1) * rows]
        return 0

    repeat(0, count, block, 0, unrolled)
    for j in range(blocks):
        at = slice(j * rows, (j + 1) * rows)
        dk = jnp.transpose(dk_s[at, :] * score_scale).astype(bf16)
        dv = jnp.transpose(dv_s[at, :]).astype(bf16)
        out_ref[j, 64:128, :] = dk
        out_ref[j, 128:192, :] = dv


def attend(qkv):
    blocks, _, rows = qkv.shape
    length = blocks * rows
    return pl.pallas_call(
        functools.partial(attend_kernel, length <= 2048),
        out_shape=(
            jax.ShapeDtypeStruct((blocks, HEAD_DIM, rows), bf16),
            jax.ShapeDtypeStruct((blocks, HEAD_DIM, rows), f32),
            jax.ShapeDtypeStruct((length // SPAN, 1, SPAN), f32),
        ),
        scratch_shapes=[
            pltpu.VMEM((length, HEAD_DIM), bf16),
            pltpu.VMEM((blocks, 1, rows), jnp.int32),
            pltpu.VMEM((2, length, SPAN), f32),
        ],
        compiler_params=pltpu.CompilerParams(vmem_limit_bytes=60 * 2**20),
        cost_estimate=estimate(
            flops=length * length * HEAD_DIM * 2,
            bytes_accessed=length * 1024,
            transcendentals=length * length // 2,
        ),
        name="attend",
    )(qkv)


def attend_back(qkv, grad, wide, lse):
    blocks, _, rows = qkv.shape
    length = blocks * rows
    return pl.pallas_call(
        functools.partial(attend_back_kernel, length <= 2048),
        out_shape=jax.ShapeDtypeStruct((blocks, 3 * HEAD_DIM, rows), bf16),
        scratch_shapes=[
            pltpu.VMEM((length, HEAD_DIM), bf16),
            pltpu.VMEM((length, HEAD_DIM), bf16),
            pltpu.VMEM((length, HEAD_DIM), bf16),
            pltpu.VMEM((length, HEAD_DIM), bf16),
            pltpu.VMEM((blocks, 1, rows), jnp.int32),
            pltpu.VMEM((blocks, 1, rows), f32),
            pltpu.VMEM((length, HEAD_DIM), f32),
            pltpu.VMEM((length, HEAD_DIM), f32),
            pltpu.VMEM((2, length, SPAN), bf16),
        ],
        compiler_params=pltpu.CompilerParams(vmem_limit_bytes=32 * 2**20),
        cost_estimate=estimate(
            flops=length * length * HEAD_DIM * 5,
            bytes_accessed=length * 2048,
            transcendentals=length * length // 2,
        ),
        name="attend_back",
    )(qkv, grad, wide, lse)


def feed_kernel(rows_ref, grad_ref, up_ref, down_ref, after_ref, out_ref, back_ref):
    step = pl.program_id(0)
    up, down = up_ref[...], down_ref[...]
    act, slope = gelu_pair(mm(rows_ref[...], up))
    out = mm(act.astype(bf16), down)
    inner = (mm(grad_ref[...], down, ((1,), (1,))) * slope).astype(bf16)
    back = mm(inner, up, ((1,), (1,)))

    @pl.when(step == 0)
    def _():
        out_ref[...] = out
        back_ref[...] = back

    @pl.when(step > 0)
    def _():
        out_ref[...] += out
        back_ref[...] += back


def feed(rows, grad, up, down, after, first, hidden):
    count, width = rows.shape
    chunk = min(hidden, 1024)
    skip = first // chunk
    whole = pl.BlockSpec((count, width), lambda c: (0, 0))
    return pl.pallas_call(
        feed_kernel,
        grid=(hidden // chunk,),
        in_specs=[
            whole,
            whole,
            pl.BlockSpec((width, chunk), lambda c: (0, c + skip)),
            pl.BlockSpec((chunk, width), lambda c: (c + skip, 0)),
            pl.BlockSpec(memory_space=pl.ANY),
        ],
        out_specs=[whole, whole],
        out_shape=[jax.ShapeDtypeStruct((count, width), f32)] * 2,
        compiler_params=pltpu.CompilerParams(vmem_limit_bytes=60 * 2**20),
        cost_estimate=estimate(
            flops=8 * count * width * hidden,
            bytes_accessed=4 * width * hidden,
            transcendentals=count * hidden,
        ),
        name="feed",
    )(rows, grad, up, down, after)


def begin_kernel(x_ref, label_ref, gain_ref, shift_ref, weight_ref, a_ref, out_ref):
    step = pl.program_id(0)
    groups = 2

    @pl.when(step == 0)
    def _():
        normed, _ = norm_stats(x_ref[...].astype(f32))
        a_ref[...] = (normed * gain_ref[...] + shift_ref[...]).astype(bf16)
        labels = label_ref[...].astype(f32).astype(bf16)
        for head in range(HEADS):
            out_ref[head, 192:208, :] = jnp.broadcast_to(labels, (16, labels.shape[1]))

    heads = HEADS // groups
    columns = jnp.transpose(mm(a_ref[...], weight_ref[...])).astype(bf16)
    at = pl.ds(pl.multiple_of(step // groups * HEAD_DIM, HEAD_DIM), HEAD_DIM)
    for head in range(heads):
        part = columns[head * HEAD_DIM : (head + 1) * HEAD_DIM]
        out_ref[step % groups * heads + head, at, :] = part


def begin(x, labels, gain, shift, weight):
    rows, width = x.shape
    return pl.pallas_call(
        begin_kernel,
        grid=(6,),
        in_specs=[
            pl.BlockSpec((rows, width), lambda c: (0, 0)),
            pl.BlockSpec((1, rows), lambda c: (0, 0)),
            pl.BlockSpec((1, width), lambda c: (0, 0)),
            pl.BlockSpec((1, width), lambda c: (0, 0)),
            pl.BlockSpec((width, width // 2), lambda c: (0, c)),
        ],
        out_specs=[
            pl.BlockSpec((rows, width), lambda c: (0, 0)),
            pl.BlockSpec((HEADS, 208, rows), lambda c: (0, 0, 0)),
        ],
        out_shape=[
            jax.ShapeDtypeStruct((rows, width), bf16),
            jax.ShapeDtypeStruct((HEADS, 208, rows), bf16),
        ],
        compiler_params=pltpu.CompilerParams(vmem_limit_bytes=60 * 2**20),
        cost_estimate=estimate(
            flops=6 * rows * width * width, bytes_accessed=6 * width * width, transcendentals=0
        ),
        name="begin",
    )(x, labels, gain, shift, weight)


def choices(logits, experts):
    lane = lax.broadcasted_iota(jnp.int32, logits.shape, 1)
    total = jnp.zeros_like(logits)
    for low, high in ((0, experts), (experts, experts + 2)):
        inside = (lane >= low) & (lane < high)
        masked = jnp.where(inside, logits, masked_score)
        e = jnp.where(inside, jnp.exp(masked - jnp.max(masked, axis=1, keepdims=True)), 0.0)
        total = total + e / jnp.sum(e, axis=1, keepdims=True)
    return total, lane


def pick(values, lane, index):
    return jnp.sum(jnp.where(lane == index, values, 0.0), axis=1, keepdims=True)


def bf16_parts(value):
    high = value.astype(bf16).astype(f32)
    rest = value - high
    middle = rest.astype(bf16).astype(f32)
    return [high, middle, rest - middle]


def middle_kernel(
    o_ref, weight_ref, x_ref, dy_ref, gain_ref, shift_ref, choose_ref, bias_ref, info_ref,
    dispatch_ref, hidden_ref, b_ref, rows_ref, slots_ref, dense_ref, scalar_ref,
):
    experts, slots, count = dispatch_ref.shape
    hidden = x_ref[...].astype(f32) + mm(o_ref[...], weight_ref[...], ((0,), (0,)))
    hidden_ref[...] = hidden
    normed, _ = norm_stats(hidden)
    b = (normed * gain_ref[...] + shift_ref[...]).astype(bf16)
    b_ref[...] = b
    rows_ref[0:count, :] = b
    dy = dy_ref[...]
    for e in range(experts):
        slots_ref[e, 0:slots, :] = mm(dispatch_ref[e], b).astype(bf16)
        slots_ref[e, slots : 2 * slots, :] = mm(dispatch_ref[e], dy).astype(bf16)
    values, lane = choices(mm(b, choose_ref[...]) + bias_ref[...], experts)
    info = info_ref[...]
    gate = pick(values, lane, info[:, 0:1].astype(jnp.int32))
    mixing = pick(values, lane, experts)
    other = pick(values, lane, experts + 1)
    scalar_ref[...] = jnp.where(lane == experts + 2, gate, values)
    dense_ref[...] = (mixing * dy.astype(f32)).astype(bf16)
    columns = bf16_parts(mixing) + bf16_parts(other * gate) + [info[:, 1:2], info[:, 1:2]]
    block = jnp.zeros_like(values)
    for k, column in enumerate(columns):
        block = jnp.where(lane == k, column, block)
    rows_ref[count:, :] = jnp.zeros((8, rows_ref.shape[1]), bf16)
    rows_ref[count:, 0:count] = jnp.transpose(block)[0:8].astype(bf16)


def middle(o, weight, x, dy, gain, shift, choose, bias, info, dispatch):
    rows, width = x.shape
    experts, slots, _ = dispatch.shape
    return pl.pallas_call(
        middle_kernel,
        out_shape=[
            jax.ShapeDtypeStruct((rows, width), f32),
            jax.ShapeDtypeStruct((rows, width), bf16),
            jax.ShapeDtypeStruct((rows + 8, width), bf16),
            jax.ShapeDtypeStruct((experts, 2 * slots, width), bf16),
            jax.ShapeDtypeStruct((rows, width), bf16),
            jax.ShapeDtypeStruct((rows, 128), f32),
        ],
        compiler_params=pltpu.CompilerParams(vmem_limit_bytes=60 * 2**20),
        cost_estimate=estimate(
            flops=4 * rows * width * width, bytes_accessed=4 * width * width, transcendentals=0
        ),
        name="middle",
    )(o, weight, x, dy, gain, shift, choose, bias, info, dispatch)


def expert_kernel(
    mine_ref, slots_ref, choose_ref, bias_ref, up_ref, down_ref, after_ref, out_ref,
    rows_s, grad_s, total_s, back_s,
):
    step = pl.program_id(0)
    sources, double, _ = slots_ref.shape
    slots = double // 2

    @pl.when(step == 0)
    def _():
        for n in range(sources):
            at = slice(n * slots, (n + 1) * slots)
            rows_s[at, :] = slots_ref[n, 0:slots, :]
            grad_s[at, :] = slots_ref[n, slots:double, :]
        values, lane = choices(mm(rows_s[...], choose_ref[...]) + bias_ref[...], sources)
        gate = pick(values, lane, mine_ref[0])
        other = pick(values, lane, sources + 1)
        grad_s[...] = (gate * (other * grad_s[...].astype(f32))).astype(bf16)
        total_s[...] = jnp.zeros_like(total_s)
        back_s[...] = jnp.zeros_like(back_s)

    up, down = up_ref[...], down_ref[...]
    act, slope = gelu_pair(mm(rows_s[...], up))
    total_s[...] += mm(act.astype(bf16), down)
    inner = (mm(grad_s[...], down, ((1,), (1,))) * slope).astype(bf16)
    back_s[...] += mm(inner, up, ((1,), (1,)))

    @pl.when(step == pl.num_programs(0) - 1)
    def _():
        for n in range(sources):
            at = slice(n * slots, (n + 1) * slots)
            out_ref[n, 0:slots, :] = total_s[at, :].astype(bf16)
            out_ref[n, slots:double, :] = back_s[at, :].astype(bf16)


def expert_feed(mine, slots, choose, bias, up, down, after):
    sources, double, width = slots.shape
    hidden = up.shape[1]
    chunk = min(hidden, 1024)
    count = sources * double // 2
    whole = pl.BlockSpec((sources, double, width), lambda c, m: (0, 0, 0))
    return pl.pallas_call(
        expert_kernel,
        grid_spec=pltpu.PrefetchScalarGridSpec(
            num_scalar_prefetch=1,
            grid=(hidden // chunk,),
            in_specs=[
                whole,
                pl.BlockSpec((width, 128), lambda c, m: (0, 0)),
                pl.BlockSpec((1, 128), lambda c, m: (0, 0)),
                pl.BlockSpec((width, chunk), lambda c, m: (0, c)),
                pl.BlockSpec((chunk, width), lambda c, m: (c, 0)),
                pl.BlockSpec(memory_space=pl.ANY),
            ],
            out_specs=whole,
            scratch_shapes=[
                pltpu.VMEM((count, width), bf16),
                pltpu.VMEM((count, width), bf16),
                pltpu.VMEM((count, width), f32),
                pltpu.VMEM((count, width), f32),
            ],
        ),
        out_shape=jax.ShapeDtypeStruct((sources, double, width), bf16),
        compiler_params=pltpu.CompilerParams(vmem_limit_bytes=60 * 2**20),
        cost_estimate=estimate(
            flops=8 * count * width * hidden,
            bytes_accessed=4 * width * hidden,
            transcendentals=count * hidden,
        ),
        name="expert_feed",
    )(mine, slots, choose, bias, up, down, after)


def combine_kernel(
    back_ref, dispatch_ref, hidden_ref, rows_ref, dy_ref, first_ref, first_back_ref, second_ref,
    second_back_ref, scalar_ref, info_ref, gain_ref, choose_ref, weight_ref,
    result_ref, grad_ref, low_ref, heads_ref, sums_ref, bias_ref,
):
    experts, slots, count = dispatch_ref.shape
    raw, grad_b = None, first_back_ref[...] + second_back_ref[...]
    for e in range(experts):
        part = mm(dispatch_ref[e], back_ref[e, 0:slots, :], ((0,), (0,)))
        raw = part if raw is None else raw + part
        grad_b = grad_b + mm(dispatch_ref[e], back_ref[e, slots : 2 * slots, :], ((0,), (0,)))
    hidden = hidden_ref[...]
    dy = dy_ref[...].astype(f32)
    scalars = scalar_ref[...]
    lane = lax.broadcasted_iota(jnp.int32, scalars.shape, 1)
    gate = pick(scalars, lane, experts + 2)
    mixing, other = pick(scalars, lane, experts), pick(scalars, lane, experts + 1)
    dense = first_ref[...] + second_ref[...]
    expert = gate * raw
    result_ref[...] = (hidden + mixing * dense + other * expert).astype(bf16)
    grad_gate = jnp.sum(other * dy * raw, axis=1, keepdims=True)
    grad_mixing = jnp.sum(dy * dense, axis=1, keepdims=True)
    grad_other = jnp.sum(dy * expert, axis=1, keepdims=True)
    mean = mixing * grad_mixing + other * grad_other
    onehot = (lane == info_ref[...][:, 0:1].astype(jnp.int32)).astype(f32)
    logits = jnp.where(lane < experts, scalars * (onehot - gate) * grad_gate, 0.0)
    logits = jnp.where(lane == experts, mixing * (grad_mixing - mean), logits)
    logits = jnp.where(lane == experts + 1, other * (grad_other - mean), logits)
    bias_ref[...] = jnp.sum(logits, axis=0, keepdims=True)
    b = rows_ref[...].astype(f32)
    sums_ref[...] = jnp.zeros_like(sums_ref)
    for e in range(experts + 2):
        column = logits[:, e : e + 1]
        grad_b = grad_b + column * choose_ref[e : e + 1, :].astype(f32)
        sums_ref[2 + e : 3 + e, :] = jnp.sum(column * b, axis=0, keepdims=True)
    normed, rstd = norm_stats(hidden)
    sums_ref[0:1, :] = jnp.sum(grad_b * normed, axis=0, keepdims=True)
    sums_ref[1:2, :] = jnp.sum(grad_b, axis=0, keepdims=True)
    grad = dy + norm_back(grad_b, gain_ref[...], normed, rstd)
    grad_ref[...] = grad
    low = grad.astype(bf16)
    low_ref[...] = low
    heads_ref[...] = mm(weight_ref[...], low, ((1,), (1,))).astype(bf16)


def combine(*operands):
    dispatch, hidden = operands[1], operands[2]
    rows, width = hidden.shape
    lines = 8 * (1 + (dispatch.shape[0] + 3) // 8)
    return pl.pallas_call(
        combine_kernel,
        out_shape=[
            jax.ShapeDtypeStruct((rows, width), bf16),
            jax.ShapeDtypeStruct((rows, width), f32),
            jax.ShapeDtypeStruct((rows, width), bf16),
            jax.ShapeDtypeStruct((width, rows), bf16),
            jax.ShapeDtypeStruct((lines, width), f32),
            jax.ShapeDtypeStruct((1, 128), f32),
        ],
        compiler_params=pltpu.CompilerParams(vmem_limit_bytes=60 * 2**20),
        cost_estimate=estimate(
            flops=4 * rows * width * width, bytes_accessed=4 * width * width, transcendentals=0
        ),
        name="combine",
    )(*operands)


def slice_kernel(
    dense_units, mine_ref, rows_ref, grad_ref, up_ref, down_ref, up_out, down_out, up_acc, down_acc
):
    step = pl.program_id(0)
    per, count = grad_ref.shape[:2]

    @pl.when(step == 0)
    def _():
        up_acc[...] = jnp.zeros_like(up_acc)
        down_acc[...] = jnp.zeros_like(down_acc)

    rows, dense_grad, expert_grad = [], [], []
    for t in range(per):
        scalars = jnp.transpose(rows_ref[t, count : count + 8, 0:count].astype(f32))
        mixing = scalars[:, 0:1] + scalars[:, 1:2] + scalars[:, 2:3]
        gate = scalars[:, 3:4] + scalars[:, 4:5] + scalars[:, 5:6]
        mine = scalars[:, 6:7] == mine_ref[0].astype(f32)
        grad = grad_ref[t].astype(f32)
        rows.append(rows_ref[t, 0:count, :])
        dense_grad.append((mixing * grad).astype(bf16))
        expert_grad.append((jnp.where(mine, gate, 0.0) * grad).astype(bf16))
    rows = jnp.concatenate(rows, axis=0)
    dense_grad = jnp.concatenate(dense_grad, axis=0)
    expert_grad = jnp.concatenate(expert_grad, axis=0)
    act, slope = gelu_pair(mm(rows, up_ref[...]))
    act = act.astype(bf16)
    inner = jnp.concatenate(
        [mm(dense_grad, down_ref[:, :dense_units]), mm(expert_grad, down_ref[:, dense_units:])],
        axis=1,
    )
    inner = (inner * slope).astype(bf16)
    first = ((0,), (0,))
    up_acc[...] += mm(inner, rows, first)
    down_acc[:dense_units, :] += mm(act[:, :dense_units], dense_grad, first)
    down_acc[dense_units:, :] += mm(act[:, dense_units:], expert_grad, first)

    @pl.when(step == pl.num_programs(0) - 1)
    def _():
        up = jnp.transpose(up_acc[...]).astype(bf16)
        own = up_out.shape[2]
        for chunk in range(up_out.shape[1]):
            lanes = up[:, chunk * 128 : (chunk + 1) * 128]
            up_out[:, chunk] = lanes.reshape(up_out.shape[0], own, 128)
        down_out[...] = down_acc[...]


def slice_grads(mine, rows, grad, up, down, dense_units, wide):
    devices, padded, width = rows.shape
    count = grad.shape[1]
    units = up.shape[1]
    per = 4
    fixed = pl.BlockSpec((width, units), lambda c, m: (0, 0))
    return pl.pallas_call(
        functools.partial(slice_kernel, dense_units),
        grid_spec=pltpu.PrefetchScalarGridSpec(
            num_scalar_prefetch=1,
            grid=(devices // per,),
            in_specs=[
                pl.BlockSpec((per, padded, width), lambda c, m: (c, 0, 0)),
                pl.BlockSpec((per, count, width), lambda c, m: (c, 0, 0)),
                fixed,
                fixed,
            ],
            out_specs=[
                pl.BlockSpec((wide, units // 128, width // wide, 128), lambda c, m: (0, 0, 0, 0)),
                pl.BlockSpec((units, width), lambda c, m: (0, 0)),
            ],
            scratch_shapes=[pltpu.VMEM((units, width), f32), pltpu.VMEM((units, width), f32)],
        ),
        out_shape=[
            jax.ShapeDtypeStruct((wide, units // 128, width // wide, 128), bf16),
            jax.ShapeDtypeStruct((units, width), f32),
        ],
        compiler_params=pltpu.CompilerParams(vmem_limit_bytes=60 * 2**20),
        cost_estimate=estimate(
            flops=8 * devices * count * width * units,
            bytes_accessed=4 * devices * count * width,
            transcendentals=devices * count * units,
        ),
        name="slice_grads",
    )(mine, rows, grad, up, down)


def product_sum(left_ref, array_ref):
    blocks, rows, width = array_ref.shape
    total = None
    for p in range(0, blocks, 2):
        left = jnp.concatenate([left_ref[p], left_ref[p + 1]], axis=1)
        part = mm(left, array_ref[p : p + 2].reshape(2 * rows, width))
        total = part if total is None else total + part
    return total


def in_kernel(left_ref, array_ref, lines_ref, out_ref):
    total = jnp.transpose(product_sum(left_ref, array_ref)).astype(bf16)
    wide, _, lanes = out_ref.shape
    own = total.shape[0] // wide
    for w in range(wide):
        rows = total[w * own : (w + 1) * own]
        out_ref[w, 0:own, :] = rows[:, 0:128]
        out_ref[w, own : own + own // 2, :] = jnp.concatenate(
            [rows[: own // 2, 128:192], rows[own // 2 :, 128:192]], axis=1
        )
        out_ref[w, own + own // 2 :, :] = lines_ref[w]


def block_products(kernel, name, out_shape, left, array, lines):
    blocks, rows, width = array.shape
    return pl.pallas_call(
        kernel,
        in_specs=[pl.BlockSpec(memory_space=pltpu.VMEM)] * 3,
        out_shape=jax.ShapeDtypeStruct(out_shape, bf16),
        compiler_params=pltpu.CompilerParams(vmem_limit_bytes=60 * 2**20),
        cost_estimate=estimate(
            flops=2 * blocks * rows * width * left.shape[1],
            bytes_accessed=2 * blocks * rows * width,
            transcendentals=0,
        ),
        name=name,
    )(left, array, lines)


def finish_kernel(
    first_ref, got_ref, got_other_ref, ups_ref, ups_other_ref, in_out, dense_out, expert_out, sum_out
):
    wide = got_ref.shape[0]
    own = in_out.shape[0]
    first = first_ref[0] == 0
    half = own // 2
    sums = None
    for w in range(wide):
        total = got_ref[w].astype(f32) + got_other_ref[w].astype(f32)
        head = w * HEAD_DIM
        in_out[:, head : head + 64] = total[:own, :64]
        in_out[:, 1024 + head : 1024 + head + 64] = total[:own, 64:]
        in_out[:half, 2048 + head : 2048 + head + 64] = total[own : own + half, :64]
        in_out[half:, 2048 + head : 2048 + head + 64] = total[own : own + half, 64:]
        small = total[own + half :]
        sums = small if sums is None else sums + small
        mine, theirs = ups_ref[w, :own].astype(f32), ups_other_ref[w].astype(f32)
        dense_out[:, w * 256 : w * 256 + 128] = jnp.where(first, mine, theirs)
        dense_out[:, w * 256 + 128 : w * 256 + 256] = jnp.where(first, theirs, mine)
        expert_out[:, w * 256 : w * 256 + 128] = ups_ref[w, own : 2 * own].astype(f32)
        expert_out[:, w * 256 + 128 : w * 256 + 256] = ups_ref[w, 2 * own :].astype(f32)
    sum_out[...] = sums


def finish(first, got, got_other, ups, ups_other, own, hidden):
    width = HEADS * HEAD_DIM
    return pl.pallas_call(
        finish_kernel,
        in_specs=[pl.BlockSpec(memory_space=pltpu.SMEM)]
        + [pl.BlockSpec(memory_space=pltpu.VMEM)] * 4,
        out_shape=[
            jax.ShapeDtypeStruct((own, 3 * width), f32),
            jax.ShapeDtypeStruct((own, hidden), f32),
            jax.ShapeDtypeStruct((own, hidden), f32),
            jax.ShapeDtypeStruct((16, 128), f32),
        ],
        compiler_params=pltpu.CompilerParams(vmem_limit_bytes=32 * 2**20),
        name="finish",
    )(first, got, got_other, ups, ups_other)


def after(value, *others):
    return lax.optimization_barrier((value,) + others)[0]


def gather(value):
    return lax.all_gather(value, WIDE, axis=0, tiled=True)


def exchange(columns):
    wide = lax.axis_size("chip") * lax.axis_size("core")
    blocks = columns.astype(bf16).reshape(wide, columns.shape[0] // wide, columns.shape[1])
    got = lax.all_to_all(blocks, WIDE, 0, 0, tiled=True)
    return got.transpose(1, 0, 2).reshape(blocks.shape[1], wide * blocks.shape[2])


def plain_slice(rows, grad, up, down):
    act, slope = gelu_pair(mm(rows, up))
    inner = (mm(grad, down, ((1,), (1,))) * slope).astype(bf16)
    return mm(rows, inner, ((0,), (0,))), mm(act.astype(bf16), grad, ((0,), (0,)))


def other_narrow(value):
    size = lax.axis_size("narrow")
    if size != 2:
        return lax.all_gather(value, "narrow", axis=0, tiled=False)
    swapped = lax.ppermute(value, "narrow", [(0, 1), (1, 0)])
    first = lax.axis_index("narrow") == 0
    return jnp.stack([jnp.where(first, value, swapped), jnp.where(first, swapped, value)])


def local(
    tokens, document, routing, capacity, load_before, first_gain, first_shift, project_in,
    project_out, second_gain, second_shift, dense_up, dense_down, router, mixer, mixer_bias,
    expert_up, expert_down, cotangent,
):
    rows, seq_count, width = tokens.shape
    assert seq_count == 1 and width == HEADS * HEAD_DIM
    chips, cores, narrow = (lax.axis_size(axis) for axis in ALL)
    wide = chips * cores
    devices = wide * narrow
    experts = capacity.shape[0]
    hidden_units = dense_up.shape[1]
    assert experts == narrow and wide % HEADS == 0 and cores == 2
    copies = wide // HEADS
    own = width // wide
    core = lax.axis_index("core")
    my_wide = lax.axis_index("chip") * cores + core
    my_narrow = lax.axis_index("narrow")
    swap = [(0, 1), (1, 0)]
    gather_all = wide == HEADS and narrow == 2

    grad_low = cotangent.reshape(rows, width)
    if gather_all:
        grad_all = lax.all_gather(grad_low, ALL, axis=0, tiled=False)

    chosen = routing.reshape(rows)
    onehot = (chosen[:, None] == jnp.arange(experts, dtype=jnp.int32)[None, :]).astype(jnp.int32)
    earlier = jnp.cumsum(onehot, axis=0) - onehot
    slot_rank = jnp.sum(earlier * onehot, axis=-1)
    kept = slot_rank < jnp.sum(capacity[None, :] * onehot, axis=-1)
    counts = jnp.sum(onehot * kept[:, None].astype(jnp.int32), axis=0)
    slots = -(-(rows * 5 // (4 * experts)) // 16) * 16
    slot_index = chosen * slots + slot_rank
    dispatch = (
        (slot_index[None, :] == jnp.arange(experts * slots, dtype=jnp.int32)[:, None])
        & kept[None, :]
    ).astype(bf16)
    dispatch = dispatch.reshape(experts, slots, rows)
    code = jnp.where(kept, chosen, experts)
    info = jnp.stack([chosen, code] + [code] * 6, axis=1).astype(f32)
    choose = jnp.concatenate([router, mixer], axis=1)
    choose = jnp.pad(choose, ((0, 0), (0, 128 - experts - 2)))
    bias = jnp.pad(mixer_bias, (experts, 126 - experts)).reshape(1, 128)

    x = tokens.reshape(rows, width)
    a, payload = begin(
        x,
        document.reshape(1, rows),
        first_gain.reshape(1, width),
        first_shift.reshape(1, width),
        project_in,
    )
    payload = jnp.repeat(payload, copies, axis=0)
    qkv = lax.all_to_all(payload, WIDE, 0, 0, tiled=True)
    expert_units, dense_units = hidden_units // wide, hidden_units // devices
    my_up = expert_up.reshape(width, hidden_units)
    my_down = expert_down.reshape(hidden_units, width)
    up_slice = lax.dynamic_slice_in_dim(my_up, my_wide * expert_units, expert_units, axis=1)
    down_slice = lax.dynamic_slice_in_dim(my_down, my_wide * expert_units, expert_units, axis=0)
    if gather_all:
        dense_first = my_wide * expert_units + my_narrow * dense_units
        dense_up_slice = lax.dynamic_slice_in_dim(dense_up, dense_first, dense_units, axis=1)
        dense_down_slice = lax.dynamic_slice_in_dim(dense_down, dense_first, dense_units, axis=0)
        ups = jnp.concatenate([dense_up_slice, up_slice], axis=1)
        downs = jnp.concatenate([dense_down_slice, down_slice], axis=0).T
        qkv = after(qkv, ups, downs)
    qkv = after(qkv, dispatch, info, choose, bias)
    head_low, head_wide, lse = attend(qkv)
    attended = lax.all_to_all(head_low, WIDE, 0, 0, tiled=True)[::copies].reshape(width, rows)

    hidden, b, rows_sent, slots_sent, dense_grad, scalars = middle(
        attended,
        project_out,
        x,
        grad_low,
        second_gain.reshape(1, width),
        second_shift.reshape(1, width),
        choose,
        bias,
        info,
        dispatch,
    )
    slots_got = lax.all_to_all(slots_sent, "narrow", 0, 0, tiled=True)
    half_units = hidden_units // 2
    dense_res, dense_back = feed(b, dense_grad, dense_up, dense_down, capacity, 0, half_units)
    if gather_all:
        rows_all = lax.all_gather(
            after(rows_sent, grad_all, slots_got, dense_res), ALL, axis=0, tiled=False
        )
    my_place = my_narrow.astype(jnp.int32).reshape(1)
    slots_back = expert_feed(my_place, slots_got, choose, bias, my_up, my_down, dense_res)
    returned = lax.all_to_all(slots_back, "narrow", 0, 0, tiled=True)
    dense_more, back_more = feed(
        b, dense_grad, dense_up, dense_down, slots_back, half_units, half_units
    )
    result, grad_hidden, grad_attn, grad_heads, second_sums, bias_part = combine(
        returned,
        dispatch,
        hidden,
        b,
        grad_low,
        dense_res,
        dense_back,
        dense_more,
        back_more,
        scalars,
        info,
        second_gain.reshape(1, width),
        choose.T,
        project_out,
    )
    result = result.reshape(rows, 1, width)

    grad_heads = grad_heads.reshape(HEADS, HEAD_DIM, rows)
    grad_heads = jnp.repeat(grad_heads, copies, axis=0)
    head_grad = lax.all_to_all(grad_heads, WIDE, 0, 0, tiled=True)
    small_part = second_sums[2 : 4 + experts].T
    bias_part = bias_part[0, experts : experts + 2]
    if gather_all:
        out_part = mm(after(attended, grad_heads), grad_attn).reshape(chips, cores, own, width)
        mine = lax.dynamic_index_in_dim(out_part, core, axis=1, keepdims=False)
        theirs = lax.dynamic_index_in_dim(out_part, 1 - core, axis=1, keepdims=False)
        out_part = mine + lax.ppermute(theirs.astype(bf16), "core", swap).astype(f32)
        out_part = out_part.reshape(chips, narrow, own // narrow, width)
        mine = lax.dynamic_index_in_dim(out_part, my_narrow, axis=1, keepdims=False)
        theirs = lax.dynamic_index_in_dim(out_part, 1 - my_narrow, axis=1, keepdims=False)
        out_part = mine + lax.ppermute(theirs.astype(bf16), "narrow", swap).astype(f32)
        head_grad = after(head_grad, out_part)
    grad_blocks = attend_back(qkv, head_grad, head_wide, lse)
    if gather_all:
        a = after(a, rows_all, grad_blocks)
    a_all = lax.all_gather(a, WIDE, axis=0, tiled=False)
    sent_back = lax.all_to_all(grad_blocks, WIDE, 0, 0, tiled=True)[::copies]

    if gather_all:
        ups_part, downs_part = slice_grads(
            my_narrow.astype(jnp.int32).reshape(1), rows_all, grad_all, ups, downs, dense_units, wide
        )
        expert_down_grad = downs_part[dense_units:].reshape(expert_units, 1, width)
        dense_down_grad = other_narrow(downs_part[:dense_units].astype(bf16)).astype(f32)
        dense_down_grad = dense_down_grad.reshape(narrow * dense_units, width)

        ups_got = lax.all_to_all(ups_part.reshape(wide, -1, 128), WIDE, 0, 0, tiled=True)
        ups_other = lax.ppermute(ups_got[:, :own], "narrow", swap)
        sent_back = after(sent_back, ups_part)

    grad_qkv = sent_back.reshape(HEADS, 3, HEAD_DIM, rows).transpose(1, 0, 2, 3)
    grad_qkv = grad_qkv.reshape(3 * width, rows)
    grad_a = mm(grad_qkv, project_in, ((0,), (1,)))
    normed_one, rstd_one = norm_stats(x.astype(f32))
    first_gain_part = jnp.sum(grad_a * normed_one, axis=0)
    first_shift_part = jnp.sum(grad_a, axis=0)
    input_grad = grad_hidden + norm_back(grad_a, first_gain, normed_one, rstd_one)
    input_grad = input_grad.astype(bf16).reshape(rows, 1, width)

    vectors = jnp.stack([first_gain_part, first_shift_part, second_sums[0], second_sums[1]])
    if gather_all:
        out_part = after(out_part, ups_part)
        chip = lax.axis_index("chip")
        for step in (1, 4, 2):
            bit = chip // step % 2
            count = out_part.shape[0] // 2
            if step == 1:
                split = out_part.reshape((count, 2) + out_part.shape[1:])
                axis = 1
            else:
                split = out_part.reshape((2, count) + out_part.shape[1:])
                axis = 0
            mine = lax.dynamic_index_in_dim(split, bit, axis=axis, keepdims=False)
            theirs = lax.dynamic_index_in_dim(split, 1 - bit, axis=axis, keepdims=False)
            pairs = [(i, i ^ step) for i in range(chips)]
            out_part = mine + lax.ppermute(theirs.astype(bf16), "chip", pairs).astype(f32)
        out_part = out_part[0].astype(bf16)
        project_out_grad = other_narrow(out_part).astype(f32).reshape(own, width)

        vectors = vectors.reshape(4, wide, own).transpose(1, 0, 2).reshape(wide, 4 * own)
        small = small_part.reshape(wide, own, experts + 2).transpose(0, 2, 1)
        small = small.reshape(wide, own * (experts + 2))
        bias_parts = jnp.stack(three_parts(bias_part)).reshape(1, 6)
        bias_parts = jnp.broadcast_to(jnp.pad(bias_parts, ((0, 0), (0, 1530))), (wide, 1536))
        flat = jnp.concatenate([vectors, small, bias_parts], axis=1).astype(bf16)
        sent = block_products(
            in_kernel, "in_grad", (wide, own * 3 // 2 + 16, 128), grad_blocks, a_all,
            flat.reshape(wide, 16, 128),
        )
        got = lax.all_to_all(after(sent, ups_got, ups_other), WIDE, 0, 0, tiled=True)
        got_other = lax.ppermute(got, "narrow", swap)
        project_in_grad, dense_up_grad, expert_up_grad, sums = finish(
            my_narrow.astype(jnp.int32).reshape(1), got, got_other, ups_got, ups_other, own, hidden_units
        )
        expert_up_grad = expert_up_grad.reshape(own, 1, hidden_units)
        sums = sums.reshape(-1)
        vector_sums = sums[: 4 * own].reshape(4, own)
        small_sum = sums[4 * own : own * (6 + experts)].reshape(experts + 2, own).T
        bias_at = own * (6 + experts)
        mixer_bias_grad = jnp.sum(sums[bias_at : bias_at + 6].reshape(3, 2), axis=0)

        codes = rows_all[:, rows + 6, :rows].astype(f32).reshape(devices * rows, 1)
        count_sum = jnp.sum((codes == jnp.arange(experts, dtype=f32)[None, :]).astype(f32), axis=0)
    else:
        def wide_sum(part):
            part = lax.psum_scatter(part.astype(bf16), WIDE, scatter_dimension=0, tiled=True)
            return lax.psum(part, "narrow").astype(f32)

        project_out_grad = wide_sum(mm(attended, grad_attn))
        dense_up_slice = lax.dynamic_slice_in_dim(
            dense_up, my_wide * expert_units, expert_units, axis=1
        )
        dense_down_slice = lax.dynamic_slice_in_dim(
            dense_down, my_wide * expert_units, expert_units, axis=0
        )
        slot_rows = slots_got[:, :slots].reshape(narrow * slots, width)
        slot_values, lane = choices(mm(slot_rows, choose) + bias, experts)
        slot_scale = pick(slot_values, lane, my_narrow), pick(slot_values, lane, experts + 1)
        slot_grads = slots_got[:, slots:].reshape(narrow * slots, width).astype(f32)
        slot_grads = (slot_scale[0] * (slot_scale[1] * slot_grads)).astype(bf16)
        dense_up_part, dense_down_part = plain_slice(
            gather(b), gather(dense_grad), dense_up_slice, dense_down_slice
        )
        dense_down_grad = lax.psum(dense_down_part.astype(bf16), "narrow").astype(f32)
        dense_up_grad = lax.psum(exchange(dense_up_part), "narrow").astype(f32)
        expert_up_part, expert_down_grad = plain_slice(
            gather(slot_rows), gather(slot_grads), up_slice, down_slice
        )
        expert_down_grad = expert_down_grad.reshape(expert_units, 1, width)
        expert_up_grad = exchange(expert_up_part).astype(f32).reshape(own, 1, hidden_units)

        flat = grad_blocks.transpose(1, 0, 2).reshape(3 * HEAD_DIM, wide * rows)
        in_part = mm(flat, a_all.reshape(wide * rows, width)).astype(bf16)
        in_part = in_part.reshape(3 * HEAD_DIM, wide, own).transpose(1, 0, 2)
        in_part = lax.all_to_all(in_part, WIDE, 0, 0, tiled=True)[::copies]
        in_part = in_part.reshape(HEADS, 3, HEAD_DIM, own).transpose(3, 1, 0, 2)
        project_in_grad = lax.psum(in_part.reshape(own, 3 * width), "narrow").astype(f32)
        vector_sums = wide_sum(vectors.T).T
        small_sum = wide_sum(small_part)
        mixer_bias_grad = lax.psum(bias_part, ALL)
        count_sum = lax.psum(counts.astype(f32), ALL)

    load_after = momentum * load_before + (1.0 - momentum) * (
        count_sum * experts / (devices * rows)
    )
    return (
        result, input_grad, vector_sums[0], vector_sums[1], project_in_grad, project_out_grad,
        vector_sums[2], vector_sums[3], dense_up_grad, dense_down_grad, small_sum[:, :experts],
        small_sum[:, experts:], mixer_bias_grad, expert_up_grad, expert_down_grad, load_after,
    )


def solution(mesh):
    wide, narrow = mesh.devices.shape
    fine = Mesh(mesh.devices.reshape(wide // 2, 2, narrow), ALL)
    by_token = P(WIDE, "narrow", None)
    by_expert = P(None, "narrow", None)
    return jax.shard_map(
        local,
        mesh=fine,
        in_specs=(
            by_token, P(WIDE, "narrow"), by_token, P(), P(), P(), P(), P(), P(), P(), P(), P(),
            P(), P(), P(), P(), by_expert, by_expert, by_token,
        ),
        out_specs=(
            by_token, by_token, P(WIDE), P(WIDE), P(WIDE, None), P(WIDE, None), P(WIDE), P(WIDE),
            P(WIDE, None), P(WIDE, None), P(WIDE, None), P(WIDE, None), P(), by_token, by_token,
            P(),
        ),
        check_vma=False,
    )
```

```python
import functools

import jax
import jax.numpy as jnp
from jax import lax
from jax.experimental import pallas as pl
from jax.experimental.pallas import tpu as pltpu
from jax.sharding import Mesh, PartitionSpec as P

HEADS = 16
HEAD_DIM = 64
WIDE = ("chip", "core")
ALL = ("chip", "core", "narrow")

SHRINK = 1
score_scale = 0.125
norm_eps = 1e-05
momentum = 0.3
masked_score = -1e30
gelu_slope = 0.7978845608028654
gelu_cubic = 0.044715

f32 = jnp.float32
bf16 = jnp.bfloat16


def mm(left, right, dims=((1,), (0,))):
    return lax.dot_general(left, right, (dims, ((), ())), preferred_element_type=f32)


def estimate(flops, bytes_accessed, transcendentals):
    return pl.CostEstimate(
        flops=flops // SHRINK,
        bytes_accessed=bytes_accessed // SHRINK,
        transcendentals=transcendentals // SHRINK,
    )


def norm_stats(rows):
    average = jnp.mean(rows, axis=-1, keepdims=True)
    centered = rows - average
    variance = jnp.mean(centered * centered, axis=-1, keepdims=True)
    rstd = lax.rsqrt(variance + norm_eps)
    return centered * rstd, rstd


def norm_back(grad, gain, normed, rstd):
    scaled = grad * gain
    mean_scaled = jnp.mean(scaled, axis=-1, keepdims=True)
    mean_product = jnp.mean(scaled * normed, axis=-1, keepdims=True)
    return rstd * (scaled - mean_scaled - normed * mean_product)


def gelu_pair(u):
    square = u * u
    t = jnp.tanh(gelu_slope * u * (1.0 + gelu_cubic * square))
    half = 0.5 * (1.0 + t)
    slope = half + 0.5 * u * (1.0 - t * t) * (gelu_slope * (1.0 + 3.0 * gelu_cubic * square))
    return u * half, slope


def three_parts(value):
    high = lax.reduce_precision(value, 8, 7)
    rest = value - high
    middle = lax.reduce_precision(rest, 8, 7)
    low = lax.reduce_precision(rest - middle, 8, 7)
    return high, middle, low


SPAN = 256
TILE = 256


def columns(ref, first, block, per):
    return jnp.concatenate(
        [ref[block * per + t, first : first + HEAD_DIM, :] for t in range(per)], axis=1
    )


def rows_of(values):
    return jnp.transpose(values.astype(f32)).astype(bf16)


def fold(tile, op):
    return op(tile.reshape(tile.shape[0] // 8, 8, tile.shape[1]), axis=0)


def repeat(low, high, body, carry, unrolled):
    if unrolled:
        for step in range(low, high):
            carry = body(step, carry)
        return carry
    return lax.fori_loop(low, high, body, carry)


def aligned(index, size):
    start = index * size
    return pl.ds(start if isinstance(index, int) else pl.multiple_of(start, size), size)


def document_starts(qkv_ref, start_s):
    labels = [qkv_ref[j, 192:208, :].astype(f32)[0:1] for j in range(qkv_ref.shape[0])]
    every = jnp.concatenate(labels, axis=0)
    counts = [jnp.sum((every < v).astype(f32), keepdims=True) for v in range(1, 5)]
    before = [jnp.zeros_like(counts[0])] + counts[:-1]
    start = sum(
        jnp.where(every >= v + 1, counts[v] - before[v], 0.0) for v in range(4)
    ).astype(jnp.int32)
    for j in range(qkv_ref.shape[0]):
        start_s[j] = start[j : j + 1]


def allowed(first_key, start, first_query, row_at, column_at, diagonal):
    keep = row_at >= start - first_key
    if diagonal is None or diagonal:
        keep = keep & (row_at - column_at <= first_query - first_key)
    return keep


def attend_kernel(unrolled, qkv_ref, low_ref, wide_ref, lse_ref, key_s, start_s, score_s):
    blocks, _, rows = qkv_ref.shape
    per = SPAN // rows
    count, ratio = blocks // per, SPAN // TILE
    for j in range(blocks):
        key_s[j * rows : (j + 1) * rows, :] = rows_of(qkv_ref[j, 64:128, :])
    document_starts(qkv_ref, start_s)
    shape = (TILE, SPAN)
    row_at = lax.broadcasted_iota(jnp.int32, shape, 0)
    column_at = lax.broadcasted_iota(jnp.int32, shape, 1)

    def block(i, _):
        query = (columns(qkv_ref, 0, i, per).astype(f32) * score_scale).astype(bf16)
        start = jnp.concatenate([start_s[i * per + t] for t in range(per)], axis=1)
        slot = i % 2

        def score(j, peak):
            at = aligned(j, TILE)
            s = mm(key_s[at, :], query)
            diagonal = j >= i * ratio if unrolled else None
            keep = allowed(j * TILE, start, i * SPAN, row_at, column_at, diagonal)
            s = jnp.where(keep, s, masked_score)
            score_s[slot, at, :] = s
            return jnp.maximum(peak, fold(s, jnp.max))

        end = (i + 1) * ratio
        peak = repeat(0, end, score, jnp.full((8, SPAN), masked_score, f32), unrolled)
        peak = jnp.max(peak, axis=0, keepdims=True)

        def weigh(j, total):
            at = aligned(j, TILE)
            e = jnp.exp(score_s[slot, at, :] - peak)
            score_s[slot, at, :] = e
            return total + fold(e, jnp.sum)

        total = repeat(0, end, weigh, jnp.zeros((8, SPAN), f32), unrolled)
        total = jnp.sum(total, axis=0, keepdims=True)
        share = 1.0 / total

        def mix(j, out):
            p = (score_s[slot, aligned(j, SPAN), :] * share).astype(bf16)
            return out + mm(columns(qkv_ref, 128, j, per), p)

        out = repeat(0, i + 1, mix, jnp.zeros((HEAD_DIM, SPAN), f32), unrolled)
        for t in range(per):
            part = out[:, t * rows : (t + 1) * rows]
            wide_ref[i * per + t] = part
            low_ref[i * per + t] = part.astype(bf16)
        lse_ref[i] = peak + jnp.log(total)
        return 0

    repeat(0, count, block, 0, unrolled)


def attend_back_kernel(
    unrolled, qkv_ref, do_ref, wide_ref, lse_ref, out_ref,
    query_s, key_s, value_s, grad_s, start_s, delta_s, dk_s, dv_s, ds_s,
):
    blocks, _, rows = qkv_ref.shape
    per = SPAN // rows
    count, ratio = blocks // per, SPAN // TILE
    for j in range(blocks):
        at = slice(j * rows, (j + 1) * rows)
        query_s[at, :] = rows_of(qkv_ref[j, 0:64, :])
        key_s[at, :] = rows_of(qkv_ref[j, 64:128, :])
        value_s[at, :] = rows_of(qkv_ref[j, 128:192, :])
        grad_s[at, :] = rows_of(do_ref[j])
        delta_s[j] = jnp.sum(do_ref[j].astype(f32) * wide_ref[j], axis=0, keepdims=True)
    document_starts(qkv_ref, start_s)
    shape = (TILE, SPAN)
    row_at = lax.broadcasted_iota(jnp.int32, shape, 0)
    column_at = lax.broadcasted_iota(jnp.int32, shape, 1)
    if not unrolled:
        dk_s[...] = jnp.zeros_like(dk_s)
        dv_s[...] = jnp.zeros_like(dv_s)

    def block(i, _):
        query = (columns(qkv_ref, 0, i, per).astype(f32) * score_scale).astype(bf16)
        grad = jnp.concatenate([do_ref[i * per + t] for t in range(per)], axis=1)
        start = jnp.concatenate([start_s[i * per + t] for t in range(per)], axis=1)
        delta = jnp.concatenate([delta_s[i * per + t] for t in range(per)], axis=1)
        lse = lse_ref[i]
        query_rows, grad_rows = query_s[aligned(i, SPAN), :], grad_s[aligned(i, SPAN), :]
        slot = i % 2

        def tile(j, dq):
            at = aligned(j, TILE)
            s = mm(key_s[at, :], query)
            diagonal = j >= i * ratio if unrolled else None
            keep = allowed(j * TILE, start, i * SPAN, row_at, column_at, diagonal)
            p = jnp.where(keep, jnp.exp(s - lse), 0.0)
            ds = (p * (mm(value_s[at, :], grad) - delta)).astype(bf16)
            p = p.astype(bf16)
            dk, dv = mm(ds, query_rows), mm(p, grad_rows)
            if unrolled and diagonal:
                dk_s[at, :] = dk
                dv_s[at, :] = dv
            else:
                dk_s[at, :] += dk
                dv_s[at, :] += dv
            ds_s[slot, at, :] = ds
            return dq

        repeat(0, (i + 1) * ratio, tile, 0, unrolled)

        def mix(j, dq):
            return dq + mm(columns(qkv_ref, 64, j, per), ds_s[slot, aligned(j, SPAN), :])

        dq = repeat(0, i + 1, mix, jnp.zeros((HEAD_DIM, SPAN), f32), unrolled)
        dq = (dq * score_scale).astype(bf16)
        for t in range(per):
            out_ref[i * per + t, 0:64, :] = dq[:, t * rows : (t + 1) * rows]
        return 0

    repeat(0, count, block, 0, unrolled)
    for j in range(blocks):
        at = slice(j * rows, (j + 1) * rows)
        dk = jnp.transpose(dk_s[at, :] * score_scale).astype(bf16)
        dv = jnp.transpose(dv_s[at, :]).astype(bf16)
        out_ref[j, 64:128, :] = dk
        out_ref[j, 128:192, :] = dv


def attend(qkv):
    blocks, _, rows = qkv.shape
    length = blocks * rows
    return pl.pallas_call(
        functools.partial(attend_kernel, length <= 2048),
        out_shape=(
            jax.ShapeDtypeStruct((blocks, HEAD_DIM, rows), bf16),
            jax.ShapeDtypeStruct((blocks, HEAD_DIM, rows), f32),
            jax.ShapeDtypeStruct((length // SPAN, 1, SPAN), f32),
        ),
        scratch_shapes=[
            pltpu.VMEM((length, HEAD_DIM), bf16),
            pltpu.VMEM((blocks, 1, rows), jnp.int32),
            pltpu.VMEM((2, length, SPAN), f32),
        ],
        compiler_params=pltpu.CompilerParams(vmem_limit_bytes=60 * 2**20),
        cost_estimate=estimate(
            flops=length * length * HEAD_DIM * 2,
            bytes_accessed=length * 1024,
            transcendentals=length * length // 2,
        ),
        name="attend",
    )(qkv)


def attend_back(qkv, grad, wide, lse):
    blocks, _, rows = qkv.shape
    length = blocks * rows
    return pl.pallas_call(
        functools.partial(attend_back_kernel, length <= 2048),
        out_shape=jax.ShapeDtypeStruct((blocks, 3 * HEAD_DIM, rows), bf16),
        scratch_shapes=[
            pltpu.VMEM((length, HEAD_DIM), bf16),
            pltpu.VMEM((length, HEAD_DIM), bf16),
            pltpu.VMEM((length, HEAD_DIM), bf16),
            pltpu.VMEM((length, HEAD_DIM), bf16),
            pltpu.VMEM((blocks, 1, rows), jnp.int32),
            pltpu.VMEM((blocks, 1, rows), f32),
            pltpu.VMEM((length, HEAD_DIM), f32),
            pltpu.VMEM((length, HEAD_DIM), f32),
            pltpu.VMEM((2, length, SPAN), bf16),
        ],
        compiler_params=pltpu.CompilerParams(vmem_limit_bytes=32 * 2**20),
        cost_estimate=estimate(
            flops=length * length * HEAD_DIM * 5,
            bytes_accessed=length * 2048,
            transcendentals=length * length // 2,
        ),
        name="attend_back",
    )(qkv, grad, wide, lse)


def feed_kernel(rows_ref, grad_ref, up_ref, down_ref, after_ref, out_ref, back_ref):
    step = pl.program_id(0)
    up, down = up_ref[...], down_ref[...]
    act, slope = gelu_pair(mm(rows_ref[...], up))
    out = mm(act.astype(bf16), down)
    inner = (mm(grad_ref[...], down, ((1,), (1,))) * slope).astype(bf16)
    back = mm(inner, up, ((1,), (1,)))

    @pl.when(step == 0)
    def _():
        out_ref[...] = out
        back_ref[...] = back

    @pl.when(step > 0)
    def _():
        out_ref[...] += out
        back_ref[...] += back


def feed(rows, grad, up, down, after, first, hidden):
    count, width = rows.shape
    chunk = min(hidden, 1024)
    skip = first // chunk
    whole = pl.BlockSpec((count, width), lambda c: (0, 0))
    return pl.pallas_call(
        feed_kernel,
        grid=(hidden // chunk,),
        in_specs=[
            whole,
            whole,
            pl.BlockSpec((width, chunk), lambda c: (0, c + skip)),
            pl.BlockSpec((chunk, width), lambda c: (c + skip, 0)),
            pl.BlockSpec(memory_space=pl.ANY),
        ],
        out_specs=[whole, whole],
        out_shape=[jax.ShapeDtypeStruct((count, width), f32)] * 2,
        compiler_params=pltpu.CompilerParams(vmem_limit_bytes=60 * 2**20),
        cost_estimate=estimate(
            flops=8 * count * width * hidden,
            bytes_accessed=4 * width * hidden,
            transcendentals=count * hidden,
        ),
        name="feed",
    )(rows, grad, up, down, after)


def begin_kernel(x_ref, label_ref, gain_ref, shift_ref, weight_ref, a_ref, out_ref):
    step = pl.program_id(0)
    groups = 2

    @pl.when(step == 0)
    def _():
        normed, _ = norm_stats(x_ref[...].astype(f32))
        a_ref[...] = (normed * gain_ref[...] + shift_ref[...]).astype(bf16)
        labels = label_ref[...].astype(f32).astype(bf16)
        for head in range(HEADS):
            out_ref[head, 192:208, :] = jnp.broadcast_to(labels, (16, labels.shape[1]))

    heads = HEADS // groups
    columns = jnp.transpose(mm(a_ref[...], weight_ref[...])).astype(bf16)
    at = pl.ds(pl.multiple_of(step // groups * HEAD_DIM, HEAD_DIM), HEAD_DIM)
    for head in range(heads):
        part = columns[head * HEAD_DIM : (head + 1) * HEAD_DIM]
        out_ref[step % groups * heads + head, at, :] = part


def begin(x, labels, gain, shift, weight):
    rows, width = x.shape
    return pl.pallas_call(
        begin_kernel,
        grid=(6,),
        in_specs=[
            pl.BlockSpec((rows, width), lambda c: (0, 0)),
            pl.BlockSpec((1, rows), lambda c: (0, 0)),
            pl.BlockSpec((1, width), lambda c: (0, 0)),
            pl.BlockSpec((1, width), lambda c: (0, 0)),
            pl.BlockSpec((width, width // 2), lambda c: (0, c)),
        ],
        out_specs=[
            pl.BlockSpec((rows, width), lambda c: (0, 0)),
            pl.BlockSpec((HEADS, 208, rows), lambda c: (0, 0, 0)),
        ],
        out_shape=[
            jax.ShapeDtypeStruct((rows, width), bf16),
            jax.ShapeDtypeStruct((HEADS, 208, rows), bf16),
        ],
        compiler_params=pltpu.CompilerParams(vmem_limit_bytes=60 * 2**20),
        cost_estimate=estimate(
            flops=6 * rows * width * width, bytes_accessed=6 * width * width, transcendentals=0
        ),
        name="begin",
    )(x, labels, gain, shift, weight)


def choices(logits, experts):
    lane = lax.broadcasted_iota(jnp.int32, logits.shape, 1)
    total = jnp.zeros_like(logits)
    for low, high in ((0, experts), (experts, experts + 2)):
        inside = (lane >= low) & (lane < high)
        masked = jnp.where(inside, logits, masked_score)
        e = jnp.where(inside, jnp.exp(masked - jnp.max(masked, axis=1, keepdims=True)), 0.0)
        total = total + e / jnp.sum(e, axis=1, keepdims=True)
    return total, lane


def pick(values, lane, index):
    return jnp.sum(jnp.where(lane == index, values, 0.0), axis=1, keepdims=True)


def bf16_parts(value):
    high = value.astype(bf16).astype(f32)
    rest = value - high
    middle = rest.astype(bf16).astype(f32)
    return [high, middle, rest - middle]


def middle_kernel(
    o_ref, weight_ref, x_ref, dy_ref, gain_ref, shift_ref, choose_ref, bias_ref, info_ref,
    dispatch_ref, hidden_ref, b_ref, rows_ref, slots_ref, dense_ref, scalar_ref,
):
    experts, slots, count = dispatch_ref.shape
    hidden = x_ref[...].astype(f32) + mm(o_ref[...], weight_ref[...], ((0,), (0,)))
    hidden_ref[...] = hidden
    normed, _ = norm_stats(hidden)
    b = (normed * gain_ref[...] + shift_ref[...]).astype(bf16)
    b_ref[...] = b
    rows_ref[0:count, :] = b
    dy = dy_ref[...]
    for e in range(experts):
        slots_ref[e, 0:slots, :] = mm(dispatch_ref[e], b).astype(bf16)
        slots_ref[e, slots : 2 * slots, :] = mm(dispatch_ref[e], dy).astype(bf16)
    values, lane = choices(mm(b, choose_ref[...]) + bias_ref[...], experts)
    info = info_ref[...]
    gate = pick(values, lane, info[:, 0:1].astype(jnp.int32))
    mixing = pick(values, lane, experts)
    other = pick(values, lane, experts + 1)
    scalar_ref[...] = jnp.where(lane == experts + 2, gate, values)
    dense_ref[...] = (mixing * dy.astype(f32)).astype(bf16)
    columns = bf16_parts(mixing) + bf16_parts(other * gate) + [info[:, 1:2], info[:, 1:2]]
    block = jnp.zeros_like(values)
    for k, column in enumerate(columns):
        block = jnp.where(lane == k, column, block)
    rows_ref[count:, :] = jnp.zeros((8, rows_ref.shape[1]), bf16)
    rows_ref[count:, 0:count] = jnp.transpose(block)[0:8].astype(bf16)


def middle(o, weight, x, dy, gain, shift, choose, bias, info, dispatch):
    rows, width = x.shape
    experts, slots, _ = dispatch.shape
    return pl.pallas_call(
        middle_kernel,
        out_shape=[
            jax.ShapeDtypeStruct((rows, width), f32),
            jax.ShapeDtypeStruct((rows, width), bf16),
            jax.ShapeDtypeStruct((rows + 8, width), bf16),
            jax.ShapeDtypeStruct((experts, 2 * slots, width), bf16),
            jax.ShapeDtypeStruct((rows, width), bf16),
            jax.ShapeDtypeStruct((rows, 128), f32),
        ],
        compiler_params=pltpu.CompilerParams(vmem_limit_bytes=60 * 2**20),
        cost_estimate=estimate(
            flops=4 * rows * width * width, bytes_accessed=4 * width * width, transcendentals=0
        ),
        name="middle",
    )(o, weight, x, dy, gain, shift, choose, bias, info, dispatch)


def expert_kernel(
    mine_ref, slots_ref, choose_ref, bias_ref, up_ref, down_ref, after_ref, out_ref,
    rows_s, grad_s, total_s, back_s,
):
    step = pl.program_id(0)
    sources, double, _ = slots_ref.shape
    slots = double // 2

    @pl.when(step == 0)
    def _():
        for n in range(sources):
            at = slice(n * slots, (n + 1) * slots)
            rows_s[at, :] = slots_ref[n, 0:slots, :]
            grad_s[at, :] = slots_ref[n, slots:double, :]
        values, lane = choices(mm(rows_s[...], choose_ref[...]) + bias_ref[...], sources)
        gate = pick(values, lane, mine_ref[0])
        other = pick(values, lane, sources + 1)
        grad_s[...] = (gate * (other * grad_s[...].astype(f32))).astype(bf16)
        total_s[...] = jnp.zeros_like(total_s)
        back_s[...] = jnp.zeros_like(back_s)

    up, down = up_ref[...], down_ref[...]
    act, slope = gelu_pair(mm(rows_s[...], up))
    total_s[...] += mm(act.astype(bf16), down)
    inner = (mm(grad_s[...], down, ((1,), (1,))) * slope).astype(bf16)
    back_s[...] += mm(inner, up, ((1,), (1,)))

    @pl.when(step == pl.num_programs(0) - 1)
    def _():
        for n in range(sources):
            at = slice(n * slots, (n + 1) * slots)
            out_ref[n, 0:slots, :] = total_s[at, :].astype(bf16)
            out_ref[n, slots:double, :] = back_s[at, :].astype(bf16)


def expert_feed(mine, slots, choose, bias, up, down, after):
    sources, double, width = slots.shape
    hidden = up.shape[1]
    chunk = min(hidden, 1024)
    count = sources * double // 2
    whole = pl.BlockSpec((sources, double, width), lambda c, m: (0, 0, 0))
    return pl.pallas_call(
        expert_kernel,
        grid_spec=pltpu.PrefetchScalarGridSpec(
            num_scalar_prefetch=1,
            grid=(hidden // chunk,),
            in_specs=[
                whole,
                pl.BlockSpec((width, 128), lambda c, m: (0, 0)),
                pl.BlockSpec((1, 128), lambda c, m: (0, 0)),
                pl.BlockSpec((width, chunk), lambda c, m: (0, c)),
                pl.BlockSpec((chunk, width), lambda c, m: (c, 0)),
                pl.BlockSpec(memory_space=pl.ANY),
            ],
            out_specs=whole,
            scratch_shapes=[
                pltpu.VMEM((count, width), bf16),
                pltpu.VMEM((count, width), bf16),
                pltpu.VMEM((count, width), f32),
                pltpu.VMEM((count, width), f32),
            ],
        ),
        out_shape=jax.ShapeDtypeStruct((sources, double, width), bf16),
        compiler_params=pltpu.CompilerParams(vmem_limit_bytes=60 * 2**20),
        cost_estimate=estimate(
            flops=8 * count * width * hidden,
            bytes_accessed=4 * width * hidden,
            transcendentals=count * hidden,
        ),
        name="expert_feed",
    )(mine, slots, choose, bias, up, down, after)


def combine_kernel(
    back_ref, dispatch_ref, hidden_ref, rows_ref, dy_ref, first_ref, first_back_ref, second_ref,
    second_back_ref, scalar_ref, info_ref, gain_ref, choose_ref, weight_ref,
    result_ref, grad_ref, low_ref, heads_ref, sums_ref, bias_ref,
):
    experts, slots, count = dispatch_ref.shape
    raw, grad_b = None, first_back_ref[...] + second_back_ref[...]
    for e in range(experts):
        part = mm(dispatch_ref[e], back_ref[e, 0:slots, :], ((0,), (0,)))
        raw = part if raw is None else raw + part
        grad_b = grad_b + mm(dispatch_ref[e], back_ref[e, slots : 2 * slots, :], ((0,), (0,)))
    hidden = hidden_ref[...]
    dy = dy_ref[...].astype(f32)
    scalars = scalar_ref[...]
    lane = lax.broadcasted_iota(jnp.int32, scalars.shape, 1)
    gate = pick(scalars, lane, experts + 2)
    mixing, other = pick(scalars, lane, experts), pick(scalars, lane, experts + 1)
    dense = first_ref[...] + second_ref[...]
    expert = gate * raw
    result_ref[...] = (hidden + mixing * dense + other * expert).astype(bf16)
    grad_gate = jnp.sum(other * dy * raw, axis=1, keepdims=True)
    grad_mixing = jnp.sum(dy * dense, axis=1, keepdims=True)
    grad_other = jnp.sum(dy * expert, axis=1, keepdims=True)
    mean = mixing * grad_mixing + other * grad_other
    onehot = (lane == info_ref[...][:, 0:1].astype(jnp.int32)).astype(f32)
    logits = jnp.where(lane < experts, scalars * (onehot - gate) * grad_gate, 0.0)
    logits = jnp.where(lane == experts, mixing * (grad_mixing - mean), logits)
    logits = jnp.where(lane == experts + 1, other * (grad_other - mean), logits)
    bias_ref[...] = jnp.sum(logits, axis=0, keepdims=True)
    b = rows_ref[...].astype(f32)
    sums_ref[...] = jnp.zeros_like(sums_ref)
    for e in range(experts + 2):
        column = logits[:, e : e + 1]
        grad_b = grad_b + column * choose_ref[e : e + 1, :].astype(f32)
        sums_ref[2 + e : 3 + e, :] = jnp.sum(column * b, axis=0, keepdims=True)
    normed, rstd = norm_stats(hidden)
    sums_ref[0:1, :] = jnp.sum(grad_b * normed, axis=0, keepdims=True)
    sums_ref[1:2, :] = jnp.sum(grad_b, axis=0, keepdims=True)
    grad = dy + norm_back(grad_b, gain_ref[...], normed, rstd)
    grad_ref[...] = grad
    low = grad.astype(bf16)
    low_ref[...] = low
    heads_ref[...] = mm(weight_ref[...], low, ((1,), (1,))).astype(bf16)


def combine(*operands):
    dispatch, hidden = operands[1], operands[2]
    rows, width = hidden.shape
    lines = 8 * (1 + (dispatch.shape[0] + 3) // 8)
    return pl.pallas_call(
        combine_kernel,
        out_shape=[
            jax.ShapeDtypeStruct((rows, width), bf16),
            jax.ShapeDtypeStruct((rows, width), f32),
            jax.ShapeDtypeStruct((rows, width), bf16),
            jax.ShapeDtypeStruct((width, rows), bf16),
            jax.ShapeDtypeStruct((lines, width), f32),
            jax.ShapeDtypeStruct((1, 128), f32),
        ],
        compiler_params=pltpu.CompilerParams(vmem_limit_bytes=60 * 2**20),
        cost_estimate=estimate(
            flops=4 * rows * width * width, bytes_accessed=4 * width * width, transcendentals=0
        ),
        name="combine",
    )(*operands)


def slice_kernel(
    dense_units, mine_ref, rows_ref, grad_ref, up_ref, down_ref, up_out, down_out, up_acc, down_acc
):
    step = pl.program_id(0)
    per, count = grad_ref.shape[:2]

    @pl.when(step == 0)
    def _():
        up_acc[...] = jnp.zeros_like(up_acc)
        down_acc[...] = jnp.zeros_like(down_acc)

    rows, dense_grad, expert_grad = [], [], []
    for t in range(per):
        scalars = jnp.transpose(rows_ref[t, count : count + 8, 0:count].astype(f32))
        mixing = scalars[:, 0:1] + scalars[:, 1:2] + scalars[:, 2:3]
        gate = scalars[:, 3:4] + scalars[:, 4:5] + scalars[:, 5:6]
        mine = scalars[:, 6:7] == mine_ref[0].astype(f32)
        grad = grad_ref[t].astype(f32)
        rows.append(rows_ref[t, 0:count, :])
        dense_grad.append((mixing * grad).astype(bf16))
        expert_grad.append((jnp.where(mine, gate, 0.0) * grad).astype(bf16))
    rows = jnp.concatenate(rows, axis=0)
    dense_grad = jnp.concatenate(dense_grad, axis=0)
    expert_grad = jnp.concatenate(expert_grad, axis=0)
    act, slope = gelu_pair(mm(rows, up_ref[...]))
    act = act.astype(bf16)
    inner = jnp.concatenate(
        [mm(dense_grad, down_ref[:, :dense_units]), mm(expert_grad, down_ref[:, dense_units:])],
        axis=1,
    )
    inner = (inner * slope).astype(bf16)
    first = ((0,), (0,))
    up_acc[...] += mm(inner, rows, first)
    down_acc[:dense_units, :] += mm(act[:, :dense_units], dense_grad, first)
    down_acc[dense_units:, :] += mm(act[:, dense_units:], expert_grad, first)

    @pl.when(step == pl.num_programs(0) - 1)
    def _():
        up = jnp.transpose(up_acc[...]).astype(bf16)
        own = up_out.shape[2]
        for chunk in range(up_out.shape[1]):
            lanes = up[:, chunk * 128 : (chunk + 1) * 128]
            up_out[:, chunk] = lanes.reshape(up_out.shape[0], own, 128)
        down_out[...] = down_acc[...]


def slice_grads(mine, rows, grad, up, down, dense_units, wide):
    devices, padded, width = rows.shape
    count = grad.shape[1]
    units = up.shape[1]
    per = 4
    fixed = pl.BlockSpec((width, units), lambda c, m: (0, 0))
    return pl.pallas_call(
        functools.partial(slice_kernel, dense_units),
        grid_spec=pltpu.PrefetchScalarGridSpec(
            num_scalar_prefetch=1,
            grid=(devices // per,),
            in_specs=[
                pl.BlockSpec((per, padded, width), lambda c, m: (c, 0, 0)),
                pl.BlockSpec((per, count, width), lambda c, m: (c, 0, 0)),
                fixed,
                fixed,
            ],
            out_specs=[
                pl.BlockSpec((wide, units // 128, width // wide, 128), lambda c, m: (0, 0, 0, 0)),
                pl.BlockSpec((units, width), lambda c, m: (0, 0)),
            ],
            scratch_shapes=[pltpu.VMEM((units, width), f32), pltpu.VMEM((units, width), f32)],
        ),
        out_shape=[
            jax.ShapeDtypeStruct((wide, units // 128, width // wide, 128), bf16),
            jax.ShapeDtypeStruct((units, width), f32),
        ],
        compiler_params=pltpu.CompilerParams(vmem_limit_bytes=60 * 2**20),
        cost_estimate=estimate(
            flops=8 * devices * count * width * units,
            bytes_accessed=4 * devices * count * width,
            transcendentals=devices * count * units,
        ),
        name="slice_grads",
    )(mine, rows, grad, up, down)


def product_sum(left_ref, array_ref):
    blocks, rows, width = array_ref.shape
    total = None
    for p in range(0, blocks, 2):
        left = jnp.concatenate([left_ref[p], left_ref[p + 1]], axis=1)
        part = mm(left, array_ref[p : p + 2].reshape(2 * rows, width))
        total = part if total is None else total + part
    return total


def in_kernel(left_ref, array_ref, lines_ref, out_ref):
    total = jnp.transpose(product_sum(left_ref, array_ref)).astype(bf16)
    wide, _, lanes = out_ref.shape
    own = total.shape[0] // wide
    for w in range(wide):
        rows = total[w * own : (w + 1) * own]
        out_ref[w, 0:own, :] = rows[:, 0:128]
        out_ref[w, own : own + own // 2, :] = jnp.concatenate(
            [rows[: own // 2, 128:192], rows[own // 2 :, 128:192]], axis=1
        )
        out_ref[w, own + own // 2 :, :] = lines_ref[w]


def block_products(kernel, name, out_shape, left, array, lines):
    blocks, rows, width = array.shape
    return pl.pallas_call(
        kernel,
        in_specs=[pl.BlockSpec(memory_space=pltpu.VMEM)] * 3,
        out_shape=jax.ShapeDtypeStruct(out_shape, bf16),
        compiler_params=pltpu.CompilerParams(vmem_limit_bytes=60 * 2**20),
        cost_estimate=estimate(
            flops=2 * blocks * rows * width * left.shape[1],
            bytes_accessed=2 * blocks * rows * width,
            transcendentals=0,
        ),
        name=name,
    )(left, array, lines)


def finish_ups_kernel(first_ref, ups_ref, ups_other_ref, dense_out, expert_out):
    wide = ups_ref.shape[0]
    own = dense_out.shape[0]
    first = first_ref[0] == 0
    for w in range(wide):
        mine, theirs = ups_ref[w, :own].astype(f32), ups_other_ref[w].astype(f32)
        dense_out[:, w * 256 : w * 256 + 128] = jnp.where(first, mine, theirs)
        dense_out[:, w * 256 + 128 : w * 256 + 256] = jnp.where(first, theirs, mine)
        expert_out[:, w * 256 : w * 256 + 128] = ups_ref[w, own : 2 * own].astype(f32)
        expert_out[:, w * 256 + 128 : w * 256 + 256] = ups_ref[w, 2 * own :].astype(f32)


def finish_ups(first, ups, ups_other, own, hidden):
    return pl.pallas_call(
        finish_ups_kernel,
        in_specs=[pl.BlockSpec(memory_space=pltpu.SMEM)]
        + [pl.BlockSpec(memory_space=pltpu.VMEM)] * 2,
        out_shape=[jax.ShapeDtypeStruct((own, hidden), f32)] * 2,
        compiler_params=pltpu.CompilerParams(vmem_limit_bytes=32 * 2**20),
        name="finish_ups",
    )(first, ups, ups_other)


def finish_kernel(got_ref, got_other_ref, in_out, *small_outs):
    wide = got_ref.shape[0]
    own = in_out.shape[0]
    half = own // 2
    sums = None
    for w in range(wide):
        total = got_ref[w].astype(f32) + got_other_ref[w].astype(f32)
        head = w * HEAD_DIM
        in_out[:, head : head + 64] = total[:own, :64]
        in_out[:, 1024 + head : 1024 + head + 64] = total[:own, 64:]
        in_out[:half, 2048 + head : 2048 + head + 64] = total[own : own + half, :64]
        in_out[half:, 2048 + head : 2048 + head + 64] = total[own : own + half, 64:]
        small = total[own + half :]
        sums = small if sums is None else sums + small
    for k in range(4):
        small_outs[k][...] = sums[k // 2 : k // 2 + 1, k % 2 * own : k % 2 * own + own]
    for k in range(2):
        line = sums[2 + k : 3 + k, :]
        small_outs[4 + k][0:1, :] = line[:, :own]
        small_outs[4 + k][1:2, :] = line[:, own:]
    bias = sums[4:5, :]
    small_outs[6][...] = bias[:, 0:2] + bias[:, 2:4] + bias[:, 4:6]


def finish(got, got_other, own):
    width = HEADS * HEAD_DIM
    return pl.pallas_call(
        finish_kernel,
        in_specs=[pl.BlockSpec(memory_space=pltpu.VMEM)] * 2,
        out_shape=[jax.ShapeDtypeStruct((own, 3 * width), f32)]
        + [jax.ShapeDtypeStruct((1, own), f32)] * 4
        + [jax.ShapeDtypeStruct((2, own), f32)] * 2
        + [jax.ShapeDtypeStruct((1, 2), f32)],
        compiler_params=pltpu.CompilerParams(vmem_limit_bytes=32 * 2**20),
        name="finish",
    )(got, got_other)


def after(value, *others):
    return lax.optimization_barrier((value,) + others)[0]


def gather(value):
    return lax.all_gather(value, WIDE, axis=0, tiled=True)


def exchange(columns):
    wide = lax.axis_size("chip") * lax.axis_size("core")
    blocks = columns.astype(bf16).reshape(wide, columns.shape[0] // wide, columns.shape[1])
    got = lax.all_to_all(blocks, WIDE, 0, 0, tiled=True)
    return got.transpose(1, 0, 2).reshape(blocks.shape[1], wide * blocks.shape[2])


def plain_slice(rows, grad, up, down):
    act, slope = gelu_pair(mm(rows, up))
    inner = (mm(grad, down, ((1,), (1,))) * slope).astype(bf16)
    return mm(rows, inner, ((0,), (0,))), mm(act.astype(bf16), grad, ((0,), (0,)))


def other_narrow(value):
    size = lax.axis_size("narrow")
    if size != 2:
        return lax.all_gather(value, "narrow", axis=0, tiled=False)
    swapped = lax.ppermute(value, "narrow", [(0, 1), (1, 0)])
    first = lax.axis_index("narrow") == 0
    return jnp.stack([jnp.where(first, value, swapped), jnp.where(first, swapped, value)])


def local(
    tokens, document, routing, capacity, load_before, first_gain, first_shift, project_in,
    project_out, second_gain, second_shift, dense_up, dense_down, router, mixer, mixer_bias,
    expert_up, expert_down, cotangent,
):
    rows, seq_count, width = tokens.shape
    assert seq_count == 1 and width == HEADS * HEAD_DIM
    chips, cores, narrow = (lax.axis_size(axis) for axis in ALL)
    wide = chips * cores
    devices = wide * narrow
    experts = capacity.shape[0]
    hidden_units = dense_up.shape[1]
    assert experts == narrow and wide % HEADS == 0 and cores == 2
    copies = wide // HEADS
    own = width // wide
    core = lax.axis_index("core")
    my_wide = lax.axis_index("chip") * cores + core
    my_narrow = lax.axis_index("narrow")
    swap = [(0, 1), (1, 0)]
    gather_all = wide == HEADS and narrow == 2

    grad_low = cotangent.reshape(rows, width)
    if gather_all:
        grad_all = lax.all_gather(grad_low, ALL, axis=0, tiled=False)

    chosen = routing.reshape(rows)
    onehot = (chosen[:, None] == jnp.arange(experts, dtype=jnp.int32)[None, :]).astype(jnp.int32)
    earlier = jnp.cumsum(onehot, axis=0) - onehot
    slot_rank = jnp.sum(earlier * onehot, axis=-1)
    kept = slot_rank < jnp.sum(capacity[None, :] * onehot, axis=-1)
    counts = jnp.sum(onehot * kept[:, None].astype(jnp.int32), axis=0)
    slots = -(-(rows * 5 // (4 * experts)) // 16) * 16
    slot_index = chosen * slots + slot_rank
    dispatch = (
        (slot_index[None, :] == jnp.arange(experts * slots, dtype=jnp.int32)[:, None])
        & kept[None, :]
    ).astype(bf16)
    dispatch = dispatch.reshape(experts, slots, rows)
    code = jnp.where(kept, chosen, experts)
    info = jnp.stack([chosen, code] + [code] * 6, axis=1).astype(f32)
    choose = jnp.concatenate([router, mixer], axis=1)
    choose = jnp.pad(choose, ((0, 0), (0, 128 - experts - 2)))
    bias = jnp.pad(mixer_bias, (experts, 126 - experts)).reshape(1, 128)

    x = tokens.reshape(rows, width)
    a, payload = begin(
        x,
        document.reshape(1, rows),
        first_gain.reshape(1, width),
        first_shift.reshape(1, width),
        project_in,
    )
    payload = jnp.repeat(payload, copies, axis=0)
    qkv = lax.all_to_all(payload, WIDE, 0, 0, tiled=True)
    expert_units, dense_units = hidden_units // wide, hidden_units // devices
    my_up = expert_up.reshape(width, hidden_units)
    my_down = expert_down.reshape(hidden_units, width)
    up_slice = lax.dynamic_slice_in_dim(my_up, my_wide * expert_units, expert_units, axis=1)
    down_slice = lax.dynamic_slice_in_dim(my_down, my_wide * expert_units, expert_units, axis=0)
    if gather_all:
        dense_first = my_wide * expert_units + my_narrow * dense_units
        dense_up_slice = lax.dynamic_slice_in_dim(dense_up, dense_first, dense_units, axis=1)
        dense_down_slice = lax.dynamic_slice_in_dim(dense_down, dense_first, dense_units, axis=0)
        ups = jnp.concatenate([dense_up_slice, up_slice], axis=1)
        downs = jnp.concatenate([dense_down_slice, down_slice], axis=0).T
        qkv = after(qkv, ups, downs)
    qkv = after(qkv, dispatch, info, choose, bias)
    head_low, head_wide, lse = attend(qkv)
    attended = lax.all_to_all(head_low, WIDE, 0, 0, tiled=True)[::copies].reshape(width, rows)

    hidden, b, rows_sent, slots_sent, dense_grad, scalars = middle(
        attended,
        project_out,
        x,
        grad_low,
        second_gain.reshape(1, width),
        second_shift.reshape(1, width),
        choose,
        bias,
        info,
        dispatch,
    )
    slots_got = lax.all_to_all(slots_sent, "narrow", 0, 0, tiled=True)
    half_units = hidden_units // 2
    dense_res, dense_back = feed(b, dense_grad, dense_up, dense_down, capacity, 0, half_units)
    if gather_all:
        rows_all = lax.all_gather(
            after(rows_sent, grad_all, slots_got, dense_res), ALL, axis=0, tiled=False
        )
    my_place = my_narrow.astype(jnp.int32).reshape(1)
    slots_back = expert_feed(my_place, slots_got, choose, bias, my_up, my_down, dense_res)
    returned = lax.all_to_all(slots_back, "narrow", 0, 0, tiled=True)
    dense_more, back_more = feed(
        b, dense_grad, dense_up, dense_down, slots_back, half_units, half_units
    )
    result, grad_hidden, grad_attn, grad_heads, second_sums, bias_part = combine(
        returned,
        dispatch,
        hidden,
        b,
        grad_low,
        dense_res,
        dense_back,
        dense_more,
        back_more,
        scalars,
        info,
        second_gain.reshape(1, width),
        choose.T,
        project_out,
    )
    result = result.reshape(rows, 1, width)

    grad_heads = grad_heads.reshape(HEADS, HEAD_DIM, rows)
    grad_heads = jnp.repeat(grad_heads, copies, axis=0)
    head_grad = lax.all_to_all(grad_heads, WIDE, 0, 0, tiled=True)
    small_part = second_sums[2 : 4 + experts].T
    bias_part = bias_part[0, experts : experts + 2]
    if gather_all:
        out_part = mm(after(attended, grad_heads), grad_attn).reshape(chips, cores, own, width)
        mine = lax.dynamic_index_in_dim(out_part, core, axis=1, keepdims=False)
        theirs = lax.dynamic_index_in_dim(out_part, 1 - core, axis=1, keepdims=False)
        out_part = mine + lax.ppermute(theirs.astype(bf16), "core", swap).astype(f32)
        out_part = out_part.reshape(chips, narrow, own // narrow, width)
        mine = lax.dynamic_index_in_dim(out_part, my_narrow, axis=1, keepdims=False)
        theirs = lax.dynamic_index_in_dim(out_part, 1 - my_narrow, axis=1, keepdims=False)
        out_part = mine + lax.ppermute(theirs.astype(bf16), "narrow", swap).astype(f32)
        head_grad = after(head_grad, out_part)
    grad_blocks = attend_back(qkv, head_grad, head_wide, lse)
    if gather_all:
        a = after(a, rows_all, grad_blocks)
    a_all = lax.all_gather(a, WIDE, axis=0, tiled=False)
    sent_back = lax.all_to_all(grad_blocks, WIDE, 0, 0, tiled=True)[::copies]

    if gather_all:
        ups_part, downs_part = slice_grads(
            my_narrow.astype(jnp.int32).reshape(1), rows_all, grad_all, ups, downs, dense_units, wide
        )
        expert_down_grad = downs_part[dense_units:].reshape(expert_units, 1, width)
        dense_down_grad = other_narrow(downs_part[:dense_units].astype(bf16)).astype(f32)
        dense_down_grad = dense_down_grad.reshape(narrow * dense_units, width)

        ups_got = lax.all_to_all(ups_part.reshape(wide, -1, 128), WIDE, 0, 0, tiled=True)
        ups_other = lax.ppermute(ups_got[:, :own], "narrow", swap)
        sent_back = after(sent_back, ups_part)

    grad_qkv = sent_back.reshape(HEADS, 3, HEAD_DIM, rows).transpose(1, 0, 2, 3)
    grad_qkv = grad_qkv.reshape(3 * width, rows)
    grad_a = mm(grad_qkv, project_in, ((0,), (1,)))
    normed_one, rstd_one = norm_stats(x.astype(f32))
    first_gain_part = jnp.sum(grad_a * normed_one, axis=0)
    first_shift_part = jnp.sum(grad_a, axis=0)
    input_grad = grad_hidden + norm_back(grad_a, first_gain, normed_one, rstd_one)
    input_grad = input_grad.astype(bf16).reshape(rows, 1, width)

    vectors = jnp.stack([first_gain_part, first_shift_part, second_sums[0], second_sums[1]])
    if gather_all:
        out_part = after(out_part, ups_part)
        chip = lax.axis_index("chip")
        for step in (1, 4, 2):
            bit = chip // step % 2
            count = out_part.shape[0] // 2
            if step == 1:
                split = out_part.reshape((count, 2) + out_part.shape[1:])
                axis = 1
            else:
                split = out_part.reshape((2, count) + out_part.shape[1:])
                axis = 0
            mine = lax.dynamic_index_in_dim(split, bit, axis=axis, keepdims=False)
            theirs = lax.dynamic_index_in_dim(split, 1 - bit, axis=axis, keepdims=False)
            pairs = [(i, i ^ step) for i in range(chips)]
            out_part = mine + lax.ppermute(theirs.astype(bf16), "chip", pairs).astype(f32)
        out_part = out_part[0].astype(bf16)
        project_out_grad = other_narrow(out_part).astype(f32).reshape(own, width)

        vectors = vectors.reshape(4, wide, own).transpose(1, 0, 2).reshape(wide, 4 * own)
        small = small_part.reshape(wide, own, experts + 2).transpose(0, 2, 1)
        small = small.reshape(wide, own * (experts + 2))
        bias_parts = jnp.stack(three_parts(bias_part)).reshape(1, 6)
        bias_parts = jnp.broadcast_to(jnp.pad(bias_parts, ((0, 0), (0, 1530))), (wide, 1536))
        flat = jnp.concatenate([vectors, small, bias_parts], axis=1).astype(bf16)
        sent = block_products(
            in_kernel, "in_grad", (wide, own * 3 // 2 + 16, 128), grad_blocks, a_all,
            flat.reshape(wide, 16, 128),
        )
        got = lax.all_to_all(after(sent, ups_got, ups_other), WIDE, 0, 0, tiled=True)
        got_other = lax.ppermute(got, "narrow", swap)
        dense_up_grad, expert_up_grad = finish_ups(
            my_narrow.astype(jnp.int32).reshape(1), ups_got, ups_other, own, hidden_units
        )
        expert_up_grad = expert_up_grad.reshape(own, 1, hidden_units)
        assert own == 64 and experts == 2
        project_in_grad, *lines = finish(got, got_other, own)
        vector_sums = [line.reshape(own) for line in lines[:4]]
        router_grad, mixer_grad = lines[4].T, lines[5].T
        mixer_bias_grad = lines[6].reshape(2)

        codes = rows_all[:, rows + 6, :rows].astype(f32).reshape(devices * rows, 1)
        count_sum = jnp.sum((codes == jnp.arange(experts, dtype=f32)[None, :]).astype(f32), axis=0)
    else:
        def wide_sum(part):
            part = lax.psum_scatter(part.astype(bf16), WIDE, scatter_dimension=0, tiled=True)
            return lax.psum(part, "narrow").astype(f32)

        project_out_grad = wide_sum(mm(attended, grad_attn))
        dense_up_slice = lax.dynamic_slice_in_dim(
            dense_up, my_wide * expert_units, expert_units, axis=1
        )
        dense_down_slice = lax.dynamic_slice_in_dim(
            dense_down, my_wide * expert_units, expert_units, axis=0
        )
        slot_rows = slots_got[:, :slots].reshape(narrow * slots, width)
        slot_values, lane = choices(mm(slot_rows, choose) + bias, experts)
        slot_scale = pick(slot_values, lane, my_narrow), pick(slot_values, lane, experts + 1)
        slot_grads = slots_got[:, slots:].reshape(narrow * slots, width).astype(f32)
        slot_grads = (slot_scale[0] * (slot_scale[1] * slot_grads)).astype(bf16)
        dense_up_part, dense_down_part = plain_slice(
            gather(b), gather(dense_grad), dense_up_slice, dense_down_slice
        )
        dense_down_grad = lax.psum(dense_down_part.astype(bf16), "narrow").astype(f32)
        dense_up_grad = lax.psum(exchange(dense_up_part), "narrow").astype(f32)
        expert_up_part, expert_down_grad = plain_slice(
            gather(slot_rows), gather(slot_grads), up_slice, down_slice
        )
        expert_down_grad = expert_down_grad.reshape(expert_units, 1, width)
        expert_up_grad = exchange(expert_up_part).astype(f32).reshape(own, 1, hidden_units)

        flat = grad_blocks.transpose(1, 0, 2).reshape(3 * HEAD_DIM, wide * rows)
        in_part = mm(flat, a_all.reshape(wide * rows, width)).astype(bf16)
        in_part = in_part.reshape(3 * HEAD_DIM, wide, own).transpose(1, 0, 2)
        in_part = lax.all_to_all(in_part, WIDE, 0, 0, tiled=True)[::copies]
        in_part = in_part.reshape(HEADS, 3, HEAD_DIM, own).transpose(3, 1, 0, 2)
        project_in_grad = lax.psum(in_part.reshape(own, 3 * width), "narrow").astype(f32)
        vector_sums = wide_sum(vectors.T).T
        small_sum = wide_sum(small_part)
        router_grad, mixer_grad = small_sum[:, :experts], small_sum[:, experts:]
        mixer_bias_grad = lax.psum(bias_part, ALL)
        count_sum = lax.psum(counts.astype(f32), ALL)

    load_after = momentum * load_before + (1.0 - momentum) * (
        count_sum * experts / (devices * rows)
    )
    return (
        result, input_grad, vector_sums[0], vector_sums[1], project_in_grad, project_out_grad,
        vector_sums[2], vector_sums[3], dense_up_grad, dense_down_grad, router_grad,
        mixer_grad, mixer_bias_grad, expert_up_grad, expert_down_grad, load_after,
    )


def solution(mesh):
    wide, narrow = mesh.devices.shape
    fine = Mesh(mesh.devices.reshape(wide // 2, 2, narrow), ALL)
    by_token = P(WIDE, "narrow", None)
    by_expert = P(None, "narrow", None)
    return jax.shard_map(
        local,
        mesh=fine,
        in_specs=(
            by_token, P(WIDE, "narrow"), by_token, P(), P(), P(), P(), P(), P(), P(), P(), P(),
            P(), P(), P(), P(), by_expert, by_expert, by_token,
        ),
        out_specs=(
            by_token, by_token, P(WIDE), P(WIDE), P(WIDE, None), P(WIDE, None), P(WIDE), P(WIDE),
            P(WIDE, None), P(WIDE, None), P(WIDE, None), P(WIDE, None), P(), by_token, by_token,
            P(),
        ),
        check_vma=False,
    )
```
